32 devices in a mesh: store: 8 (over z, x), tp: 4 (over y, core).
Axes of the slice: x: 2, y: 2, z: 4, core: 2. Of those that a mesh axis runs over, the one named last changes fastest.
Arguments:
- kv_store: bfloat16 [24, 2, 256, 512], P('store', None, None, 'tp'), may hold values from -6 to 6
- kv_scale: bfloat16 [24, 2, 4, 2], P('store', None, 'tp'), may hold values from 0.25 to 40
- span_home: int32 [24], replicated, may hold values from 0 to 23, as said below
- doc_ids: int32 [8, 20], P('store'), may hold values from 0 to 23, as said below
- doc_count: int32 [8], P('store'), may hold values from 6 to 20, as said below
- recompute_rows: int32 [8, 4, 128], P('store'), may hold values from 0 to 5119, as said below
- query_len: int32 [8], P('store'), may hold values from 1 to 256, as said below
- hidden: bfloat16 [8, 768, 4096], P('store', None, 'tp'), may hold values from -400 to 400
- norm_gain: bfloat16 [4096], replicated, may hold values from 0.5 to 1.5
- w_q: bfloat16 [4096, 2048], P(None, 'tp'), may hold values from -0.09375 to 0.09375
- w_kv: bfloat16 [4096, 2, 512], P(None, None, 'tp'), may hold values from -0.09375 to 0.09375
Outputs:
- attn_out: bfloat16 [8, 256, 2048], P('store', None, 'tp')
- context_kv: bfloat16 [8, 2, 5120, 512], P('store', None, None, 'tp')
The draws below stay inside these ranges and needn't reach their ends.
Inputs may be any that keep to these rules, and one draw needn't show every extreme that they name: `span_home`: each storage position occurs once; position p lies on index p // 3 of store. `doc_ids`: the 20 ids of a request are distinct; the first doc_count are its documents; a request's ids name at most 3 spans stored on one index of store, and exactly 3 on some index. `doc_count`: some request has 20 documents. `recompute_rows`: distinct within a request and below doc_count * 256. `query_len`: some request has 256 query tokens.
All inputs are finite; a program needn't handle non-finite values.
Results may differ from the reference program's by a relative error of at most 0.015.
The reference program's roundings to bfloat16 on the way (of `cached`, `normed` and `weights`) count: a program that leaves them out, or rounds other values in their place, can miss the bound.
Values may be sent and summed in bfloat16 or wider, within the bound.
A program may use at most 128 MiB of HBM per device.

```python
import math
import jax
import jax.numpy as jnp
from jax import lax

D = 4096
HD = 128
QH_DEV = 4
KVH = 4
QHEADS = 16
SPAN = 256
SB = 128
NB = 2
MAXDOC = 20
MINDOC = 6
CH_DEV = 3
SPANS = 24
CAP = 3
RB = 4
RBROWS = 128
QLEN = 256
ROWS = 768
CTXMAX = 5120
REQUESTS = 8
N_STORE = 8


def placement_order(key):
    key = jax.random.fold_in(key, 100)
    return jax.random.permutation(key, SPANS).astype(jnp.int32)


def request_counts(key):
    key = jax.random.fold_in(key, 101)
    key_one, key_two = jax.random.split(key)
    counts = jax.random.randint(key_one, (REQUESTS,), MINDOC, MAXDOC + 1)
    fullest = jax.random.randint(key_two, (), 0, REQUESTS)
    return jnp.where(jnp.arange(REQUESTS) == fullest, MAXDOC, counts).astype(jnp.int32)


def draw_span_home(key, part):
    order = placement_order(key)
    return order


def draw_doc_count(key, part):
    counts = request_counts(key)
    return counts


def draw_doc_ids(key, part):
    order = placement_order(key)
    counts = request_counts(key)
    key = jax.random.fold_in(key, 5)
    key_one, key_two, key_three, key_four = jax.random.split(key, 4)
    entries = N_STORE * CAP
    owner_dev = jnp.arange(entries) // CAP
    copy_rank = jnp.arange(entries) % CAP
    weights = jax.random.randint(key_one, (N_STORE,), 1, 9)
    raw_bits = jax.random.randint(key_two, (REQUESTS, entries), 0, 2 ** 20)
    scores = raw_bits // weights[owner_dev][None, :] * 256 + jnp.arange(entries)[None, :]
    leader = owner_dev[jnp.argmin(scores, axis=1)]
    scores = jnp.where(owner_dev[None, :] == leader[:, None], copy_rank[None, :] - CAP, scores)
    ranked = jnp.argsort(scores, axis=1)[:, :MAXDOC]
    shuffle_bits = jax.random.randint(key_three, (REQUESTS, MAXDOC), 0, 2 ** 20) * 64 + jnp.arange(MAXDOC)[None, :]
    live_slots = jnp.arange(MAXDOC)[None, :] < counts[:, None]
    shuffle_bits = jnp.where(live_slots, shuffle_bits, 2 ** 27 + jnp.arange(MAXDOC)[None, :])
    chosen = jnp.take_along_axis(ranked, jnp.argsort(shuffle_bits, axis=1), axis=1)
    chosen_dev = owner_dev[chosen]
    chosen_copy = copy_rank[chosen]
    base_slot = jax.random.randint(key_four, (REQUESTS, N_STORE), 0, CH_DEV)
    slot_index = (jnp.take_along_axis(base_slot, chosen_dev, axis=1) + chosen_copy) % CH_DEV
    storage_pos = chosen_dev * CH_DEV + slot_index
    inverse = jnp.argsort(order)
    return inverse[storage_pos].astype(jnp.int32)


def draw_recompute_rows(key, part):
    counts = request_counts(key)
    key = jax.random.fold_in(key, 7)
    raw_bits = jax.random.randint(key, (REQUESTS, CTXMAX), 0, 2 ** 17)
    scores = raw_bits * 8192 + jnp.arange(CTXMAX)[None, :]
    live_rows = jnp.arange(CTXMAX)[None, :] < counts[:, None] * SPAN
    scores = jnp.where(live_rows, scores, 2 ** 30 + jnp.arange(CTXMAX)[None, :])
    picked = jnp.argsort(scores, axis=1)[:, :RB * RBROWS]
    return picked.reshape(REQUESTS, RB, RBROWS).astype(jnp.int32)


def draw_query_len(key, part):
    key = jax.random.fold_in(key, 9)
    key_one, key_two = jax.random.split(key)
    lengths = jax.random.randint(key_one, (REQUESTS,), 1, QLEN + 1)
    fullest = jax.random.randint(key_two, (), 0, REQUESTS)
    return jnp.where(jnp.arange(REQUESTS) == fullest, QLEN, lengths).astype(jnp.int32)


def draw_kv_scale(key, part):
    key = jax.random.fold_in(key, 11)
    key_one = jax.random.fold_in(key, 0)
    shape_all = (SPANS, 2, KVH, NB)
    scales = jnp.exp(jax.random.uniform(key_one, shape_all, jnp.float32, math.log(0.25), math.log(3.0)))
    return scales.astype(jnp.bfloat16)


def draw_hidden(key, part):
    key = jax.random.fold_in(key, 13)
    key_one, key_two, key_three = jax.random.split(key, 3)
    shape_all = (REQUESTS, ROWS, D)
    row_scale = jnp.exp(jax.random.uniform(key_one, (REQUESTS, ROWS, 1), jnp.float32, 0.0, math.log(10.0)))
    column_scale = jnp.exp(jax.random.uniform(key_two, (1, 1, D), jnp.float32, 0.0, math.log(10.0)))
    values = jnp.clip(jax.random.normal(key_three, shape_all, jnp.float32), -4.0, 4.0)
    return (values * row_scale * column_scale).astype(jnp.bfloat16)


def block_scale(stream_key, shape, shards, low, largest):
    loudness, own = 1.0, jax.random.fold_in(stream_key, 6)
    for dim, blocks in shards:
        steps = jnp.exp(jax.random.uniform(jax.random.fold_in(own, dim), (blocks,), jnp.float32, low / len(shards), largest / len(shards)))
        loudness = loudness * jnp.repeat(steps, shape[dim] // blocks).reshape([-1 if axis == dim else 1 for axis in range(len(shape))])
    return loudness


def centred(own_key, extent, deviation, limit, cuts=(), held_as=jnp.bfloat16):
    result = jax.random.normal(own_key, extent, jnp.float32) * deviation
    if len(cuts) > 0:
        result = block_scale(own_key, extent, cuts, -0.22, 0.18) * result
    return jnp.clip(result, min=-limit, max=limit).astype(held_as)


def setup_inputs(seed: int = 0) -> dict:
    key_of = jax.random.split(jax.random.key(seed), 12)
    kv_store = centred(key_of[0], (SPANS, 2, SPAN, KVH * HD), 1.0, 6.0, ((0, 8), (3, 4)))
    kv_scale = draw_kv_scale(jax.random.fold_in(key_of[11], 71), 0)
    span_home = draw_span_home(jax.random.fold_in(key_of[11], 71), 0)
    doc_ids = draw_doc_ids(jax.random.fold_in(key_of[11], 71), 0)
    doc_count = draw_doc_count(jax.random.fold_in(key_of[11], 71), 0)
    recompute_rows = draw_recompute_rows(jax.random.fold_in(key_of[11], 71), 0)
    query_len = draw_query_len(jax.random.fold_in(key_of[11], 71), 0)
    hidden = draw_hidden(jax.random.fold_in(key_of[11], 71), 0)
    norm_gain = jnp.clip(1.0 + 0.1 * jax.random.normal(key_of[8], (D,), jnp.float32), 0.5, 1.5).astype(jnp.bfloat16)
    w_q = centred(key_of[9], (D, QHEADS * HD), D ** -0.5, 0.09375, ((1, 4),))
    w_kv = centred(key_of[10], (D, 2, KVH * HD), D ** -0.5, 0.09375, ((2, 4),))
    return {"kv_store": kv_store, "kv_scale": kv_scale, "span_home": span_home, "doc_ids": doc_ids, "doc_count": doc_count, "recompute_rows": recompute_rows, "query_len": query_len, "hidden": hidden, "norm_gain": norm_gain, "w_q": w_q, "w_kv": w_kv}


rope_base = 500000.0
norm_eps = 1e-05

def rope_angles(positions, head_width):
    halfway = head_width // 2
    exponent = jnp.arange(halfway, dtype=jnp.float32) * (2.0 / head_width)
    inverse_freq = jnp.power(jnp.float32(rope_base), -exponent)
    angles = positions.astype(jnp.float32)[:, None] * inverse_freq[None, :]
    return (jnp.cos(angles), jnp.sin(angles))

def rotate_half(values, cosine, sine_part):
    halfway = values.shape[-1] // 2
    low_half = values[..., :halfway]
    high_half = values[..., halfway:]
    return jnp.concatenate([low_half * cosine - high_half * sine_part, high_half * cosine + low_half * sine_part], axis=-1)

def reference(kv_store, kv_scale, span_home, doc_ids, doc_count, recompute_rows, query_len, hidden, norm_gain, w_q, w_kv):
    recompute_total = RB * RBROWS
    context_max = MAXDOC * SPAN
    kv_heads = KVH

    def one_request(request):
        doc_list, doc_total, recompute_pos, query_total, layer_input = request
        position = span_home[doc_list]
        codes = kv_store[position].astype(jnp.float32).reshape(MAXDOC, 2, SPAN, kv_heads, HD)
        scales = jnp.repeat(kv_scale[position].astype(jnp.float32), SB, axis=3)
        scales = jnp.transpose(scales, (0, 1, 3, 2))
        dequant = codes * scales[..., None]
        shift_cos, shift_sin = rope_angles(jnp.arange(MAXDOC, dtype=jnp.int32) * SPAN, HD)
        cached_keys = rotate_half(dequant[:, 0], shift_cos[:, None, None, :], shift_sin[:, None, None, :])
        cached = jnp.stack([cached_keys, dequant[:, 1]], axis=0).reshape(2, context_max, kv_heads * HD)
        live_rows = jnp.arange(context_max) < doc_total * SPAN
        cached = jnp.where(live_rows[None, :, None], cached, 0.0).astype(jnp.bfloat16)
        features = layer_input.astype(jnp.float32)
        inverse_rms = lax.rsqrt(lax.optimization_barrier(jnp.mean(features * features, axis=-1, keepdims=True)) + norm_eps)
        normed = (features * inverse_rms * norm_gain.astype(jnp.float32)).astype(jnp.bfloat16)
        query_proj = jnp.dot(normed[recompute_total:], w_q, preferred_element_type=jnp.float32)
        kv_proj = jnp.dot(normed, w_kv.reshape(D, 2 * kv_heads * HD), preferred_element_type=jnp.float32)
        kv_proj = kv_proj.reshape(-1, 2, kv_heads, HD)
        flat_pos = recompute_pos.reshape(recompute_total).astype(jnp.int32)
        query_pos = doc_total * SPAN + jnp.arange(QLEN, dtype=jnp.int32)
        row_cos, row_sin = rope_angles(jnp.concatenate([flat_pos, query_pos.astype(jnp.int32)]), HD)
        new_keys = rotate_half(kv_proj[:, 0], row_cos[:, None, :], row_sin[:, None, :]).astype(jnp.bfloat16)
        new_values = kv_proj[:, 1].astype(jnp.bfloat16)
        queries = rotate_half(query_proj.reshape(QLEN, QHEADS, HD), row_cos[recompute_total:, None, :], row_sin[recompute_total:, None, :]).astype(jnp.bfloat16)
        patched = cached.at[0, flat_pos].set(new_keys[:recompute_total].reshape(recompute_total, kv_heads * HD))
        patched = patched.at[1, flat_pos].set(new_values[:recompute_total].reshape(recompute_total, kv_heads * HD))
        all_keys = jnp.concatenate([patched[0].reshape(context_max, kv_heads, HD), new_keys[recompute_total:]], axis=0)
        all_values = jnp.concatenate([patched[1].reshape(context_max, kv_heads, HD), new_values[recompute_total:]], axis=0)
        query_index = jnp.arange(QLEN)
        key_index = jnp.arange(context_max + QLEN)
        allowed = jnp.where(key_index[None, :] < context_max, (key_index < doc_total * SPAN)[None, :], key_index[None, :] - context_max <= query_index[:, None])
        head_queries = jnp.transpose(queries.reshape(QLEN, kv_heads, QH_DEV, HD), (1, 2, 0, 3))
        head_keys = jnp.transpose(all_keys, (1, 0, 2))
        head_values = jnp.transpose(all_values, (1, 0, 2))

        def one_head(inputs):
            group_queries, group_keys, group_values = inputs
            scores = jnp.einsum('hqd,kd->hqk', group_queries.astype(jnp.float32), group_keys.astype(jnp.float32)) * HD ** (-0.5)
            scores = jnp.where(allowed[None], scores, -jnp.inf)
            top_score = lax.optimization_barrier(jnp.max(scores, axis=-1, keepdims=True))
            exp_terms = jnp.where(allowed[None], jnp.exp(scores - top_score), 0.0)
            weights = (exp_terms / lax.optimization_barrier(jnp.sum(exp_terms, axis=-1, keepdims=True))).astype(jnp.bfloat16)
            return jnp.einsum('hqk,kd->hqd', weights.astype(jnp.float32), group_values.astype(jnp.float32))
        mixed_heads = lax.map(one_head, (head_queries, head_keys, head_values))
        mixed_rows = jnp.transpose(mixed_heads, (2, 0, 1, 3)).reshape(QLEN, QHEADS * HD)
        mixed_rows = jnp.where((query_index < query_total)[:, None], mixed_rows, 0.0)
        return (mixed_rows.astype(jnp.bfloat16), patched)
    attn_out, context_kv = lax.map(one_request, (doc_ids, doc_count, recompute_rows, query_len, hidden))
    return (attn_out, context_kv)
```

```python
import functools

import jax
import jax.numpy as jnp
import numpy as np
from jax import lax
from jax.experimental import pallas as pl
from jax.experimental.pallas import tpu as pltpu
from jax.sharding import PartitionSpec as P

SPAN = 256
SB = 128
MAXDOC = 20
HEAD = 128
HALF = HEAD // 2
CHUNK = 128
SCALE_ROWS = 16
rope_base = 500000.0
norm_eps = 1e-05
f32, bf16 = jnp.float32, jnp.bfloat16
MESH = pl.DeviceIdType.MESH
ANY = pl.BlockSpec(memory_space=pl.ANY)
VMEM = pl.BlockSpec(memory_space=pltpu.VMEM)
SMEM = pl.BlockSpec(memory_space=pltpu.SMEM)


def inverse_freq():
    half = np.power(rope_base, -np.arange(HALF) * (2.0 / HEAD)).astype(np.float32)
    return np.concatenate([half, half])


def rotate(values, cosine, signed_sine):
    return values * cosine + pltpu.roll(values, HALF, 1) * signed_sine


def gather_kernel(
    hidden, codes, scales, w_q, w_kv, gain, angles,
    q_out, k_out, v_out, codes_out, scales_out,
    hid, wq, wkv_raw, wkv, wide,
    local_sem, hid_send, hid_recv, up_send, down_send, x_send, z_recv, x_recv,
):
    s = lax.axis_index("store")
    t = lax.axis_index("tp")
    z, x = s // 2, s % 2
    y, c = t // 2, t % 2
    last = 3
    across = (1 - y) * 2 + c
    sibling = y * 2 + (1 - c)
    diagonal = (1 - y) * 2 + (1 - c)
    x_peer = z * 2 + (1 - x)

    barrier = pltpu.get_barrier_semaphore()

    def greet(axis, index):
        pl.semaphore_signal(barrier, inc=1, device_id={axis: index}, device_id_type=MESH)

    greet("tp", across)
    greet("tp", sibling)
    greet("store", x_peer)
    pl.when(z > 0)(lambda: greet("store", s - 2))
    pl.when(z < last)(lambda: greet("store", s + 2))
    pl.semaphore_wait(barrier, 3 + jnp.where(z > 0, 1, 0) + jnp.where(z < last, 1, 0))

    def span_copies(own, owner_z, column, send, recv, target):
        slot = owner_z * 2 + column
        pairs = ((codes if own else codes_out.at[slot], codes_out.at[slot], 0),
                 (scales if own else scales_out.at[slot], scales_out.at[slot], 1))
        return [
            pltpu.make_async_remote_copy(
                src_ref=src, dst_ref=dst, send_sem=send.at[owner_z, i], recv_sem=recv.at[owner_z, i],
                device_id={"store": target}, device_id_type=MESH,
            )
            for src, dst, i in pairs
        ]

    def start_all(copies):
        for copy in copies:
            copy.start()

    def up(own, owner_z):
        return span_copies(own, owner_z, x, up_send, z_recv, s + 2)

    def down(own, owner_z):
        return span_copies(own, owner_z, x, down_send, z_recv, s - 2)

    def over(own, owner_z):
        return span_copies(own, owner_z, x, x_send, x_recv, x_peer)

    def hidden_copy(kind, chunk):
        rows = pl.ds(chunk * CHUNK, CHUNK)
        slot = across if kind == 2 else t
        return pltpu.make_async_remote_copy(
            src_ref=hid.at[slot, rows] if kind == 2 else hidden.at[rows],
            dst_ref=hid.at[slot, rows],
            send_sem=hid_send.at[kind, chunk], recv_sem=hid_recv.at[kind, chunk],
            device_id={"tp": across if kind == 0 else sibling}, device_id_type=MESH,
        )

    def hidden_arrival(kind, chunk):
        rows = pl.ds(chunk * CHUNK, CHUNK)
        slot = (across, sibling, diagonal)[kind]
        pltpu.make_async_remote_copy(
            src_ref=hidden.at[rows], dst_ref=hid.at[slot, rows],
            send_sem=hid_send.at[kind, chunk], recv_sem=hid_recv.at[kind, chunk],
            device_id={"tp": across if kind == 0 else sibling}, device_id_type=MESH,
        ).wait_recv()

    chunks = hidden.shape[0] // CHUNK
    query_chunks = q_out.shape[1] // CHUNK
    order = list(range(chunks - query_chunks, chunks)) + list(range(chunks - query_chunks))

    pl.when(z < last)(lambda: start_all(up(True, z)))
    pl.when(z > 0)(lambda: start_all(down(True, z)))
    start_all(over(True, z))
    for chunk in order:
        hidden_copy(0, chunk).start()
    for chunk in order:
        hidden_copy(1, chunk).start()
    local = [
        pltpu.make_async_copy(w_kv, wkv_raw, local_sem.at[0]),
        pltpu.make_async_copy(w_q, wq, local_sem.at[1]),
        pltpu.make_async_copy(hidden, hid.at[t], local_sem.at[2]),
        pltpu.make_async_copy(codes, codes_out.at[s], local_sem.at[3]),
        pltpu.make_async_copy(scales, scales_out.at[s], local_sem.at[4]),
    ]
    start_all(local)
    local[0].wait()
    block = wide.shape[0]

    def split_pairs(i, carry):
        wide[...] = wkv_raw[pl.ds(pl.multiple_of(i * block, block), block), :].astype(f32)
        rows = pl.ds(pl.multiple_of(i * (block // 2), block // 2), block // 2)
        wkv[rows, 0:HEAD] = wide[pl.ds(0, block // 2, stride=2), :].astype(bf16)
        wkv[rows, HEAD:2 * HEAD] = wide[pl.ds(1, block // 2, stride=2), :].astype(bf16)
        return carry

    lax.fori_loop(0, wkv_raw.shape[0] // block, split_pairs, 0)
    for copy in local[1:]:
        copy.wait()

    parts, _, width = hid.shape

    def project(chunk):
        rows = pl.ds(chunk * CHUNK, CHUNK)
        squares = jnp.zeros((CHUNK, 1), f32)
        for part in range(parts):
            values = hid[part, rows, :].astype(f32)
            squares = squares + jnp.sum(values * values, axis=1, keepdims=True)
        inverse_rms = lax.rsqrt(squares * (1.0 / (parts * width)) + norm_eps)
        kv = jnp.zeros((CHUNK, 2 * HEAD), f32)
        is_query = chunk >= chunks - query_chunks
        q = jnp.zeros((CHUNK, wq.shape[1]), f32)
        for part in range(parts):
            columns = pl.ds(part * width, width)
            normed = (hid[part, rows, :].astype(f32) * inverse_rms * gain[:, columns]).astype(bf16)
            kv = kv + jnp.dot(normed, wkv[columns, :], preferred_element_type=f32)
            if is_query:
                q = q + jnp.dot(normed, wq[columns, :], preferred_element_type=f32)
        angle = angles[rows, :]
        cosine = jnp.cos(angle)
        lane = lax.broadcasted_iota(jnp.int32, angle.shape, 1)
        sine = jnp.sin(angle)
        sine = jnp.where(lane < HALF, -sine, sine)
        k_out[rows, :] = rotate(kv[:, :HEAD], cosine, sine)
        v_out[rows, :] = kv[:, HEAD:]
        if is_query:
            q_rows = pl.ds((chunk - (chunks - query_chunks)) * CHUNK, CHUNK)
            for g in range(q_out.shape[0]):
                q_out[g, q_rows, :] = rotate(q[:, g * HEAD:(g + 1) * HEAD], cosine, sine).astype(bf16)

    def span_step(k):
        @pl.when(z >= k)
        def _():
            for copy in up(False, z - k):
                copy.wait_recv()
            pl.when(z < last)(lambda: start_all(up(False, z - k)))
            start_all(over(False, z - k))

        @pl.when(z + k <= last)
        def _():
            for copy in down(False, z + k):
                copy.wait_recv()
            pl.when(z > 0)(lambda: start_all(down(False, z + k)))
            start_all(over(False, z + k))

    hooks = {0: 1, 2: 2, 3: 3}
    for i in range(chunks + 1):
        if i < chunks:
            hidden_arrival(0, order[i])
            hidden_copy(2, order[i]).start()
        if i in hooks:
            span_step(hooks[i])
        if i > 0:
            hidden_arrival(1, order[i - 1])
            hidden_arrival(2, order[i - 1])
            project(order[i - 1])

    for owner in range(4):
        for copy in span_copies(False, owner, 1 - x, x_send, x_recv, x_peer):
            copy.wait_recv()
    for chunk in range(chunks):
        for kind in range(3):
            hidden_copy(kind, chunk).wait_send()
    for owner in range(4):
        for copy in over(False, owner):
            copy.wait_send()

        @pl.when(jnp.logical_and(z < last, owner <= z))
        def _():
            for copy in up(False, owner):
                copy.wait_send()

        @pl.when(jnp.logical_and(z > 0, owner >= z))
        def _():
            for copy in down(False, owner):
                copy.wait_send()


def gather_and_project(peers, tp, hidden, codes, scales, w_q, w_kv, gain, angles):
    rows, width = hidden.shape
    features = w_q.shape[0]
    heads = w_q.shape[1] // HEAD
    chunks = rows // CHUNK
    return pl.pallas_call(
        gather_kernel,
        out_shape=(
            jax.ShapeDtypeStruct((heads, SPAN, HEAD), bf16),
            jax.ShapeDtypeStruct((rows, HEAD), f32),
            jax.ShapeDtypeStruct((rows, HEAD), f32),
            jax.ShapeDtypeStruct((peers,) + codes.shape, bf16),
            jax.ShapeDtypeStruct((peers,) + scales.shape, bf16),
        ),
        in_specs=[ANY, ANY, ANY, ANY, ANY, VMEM, VMEM],
        out_specs=(VMEM, VMEM, VMEM, ANY, ANY),
        scratch_shapes=[
            pltpu.VMEM((tp, rows, width), bf16),
            pltpu.VMEM((features, w_q.shape[1]), bf16),
            pltpu.VMEM((2 * features, HEAD), bf16),
            pltpu.VMEM((features, 2 * HEAD), bf16),
            pltpu.VMEM((512, HEAD), f32),
            pltpu.SemaphoreType.DMA((5,)),
            pltpu.SemaphoreType.DMA((3, chunks)),
            pltpu.SemaphoreType.DMA((3, chunks)),
            pltpu.SemaphoreType.DMA((4, 2)),
            pltpu.SemaphoreType.DMA((4, 2)),
            pltpu.SemaphoreType.DMA((4, 2)),
            pltpu.SemaphoreType.DMA((4, 2)),
            pltpu.SemaphoreType.DMA((4, 2)),
        ],
        compiler_params=pltpu.CompilerParams(
            collective_id=0, has_side_effects=True, vmem_limit_bytes=48 * 2**20
        ),
        name="gather_project",
    )(hidden, codes, scales, w_q, w_kv, gain, angles)


def plain_gather_and_project(hidden, codes, scales, w_q, w_kv, gain, angles):
    rows = hidden.shape[0]
    heads = w_q.shape[1] // HEAD
    all_codes = lax.all_gather(codes, "store", axis=0)
    all_scales = lax.all_gather(scales, "store", axis=0)
    features = lax.all_gather(hidden, "tp", axis=1, tiled=True).astype(f32)
    inverse_rms = lax.rsqrt(jnp.mean(features * features, axis=-1, keepdims=True) + norm_eps)
    normed = (features * inverse_rms * gain).astype(bf16)
    cosine, sine = jnp.cos(angles), jnp.sin(angles)
    sine = jnp.where(jnp.arange(HEAD)[None, :] < HALF, -sine, sine)
    kv = jnp.dot(normed, w_kv.reshape(-1, 2 * HEAD), preferred_element_type=f32)
    q = jnp.dot(normed[rows - SPAN:], w_q, preferred_element_type=f32)
    q = jnp.transpose(q.reshape(SPAN, heads, HEAD), (1, 0, 2))

    def turn(values, cosine, sine):
        return values * cosine + jnp.roll(values, HALF, axis=-1) * sine

    new_keys = turn(kv[:, :HEAD], cosine, sine)
    q = turn(q, cosine[rows - SPAN:], sine[rows - SPAN:]).astype(bf16)
    return q, new_keys, kv[:, HEAD:], all_codes, all_scales


def attend_kernel(
    stored, home, ids, count, recompute, query_len, codes, scales, doc_cos, doc_sin, q, new_k, new_v,
    out, context,
    fetched, scale_rows, key_rows, value_rows, keys, values, scores, top, total, mixed, fetch_sem, out_sem,
):
    docs = count[0]
    recompute_total = recompute.shape[0]
    context_max = MAXDOC * SPAN
    heads = q.shape[0]

    def fetch(j):
        position = home[ids[0, j]]
        return pltpu.make_async_copy(codes.at[position], fetched.at[j], fetch_sem.at[j])

    lax.fori_loop(0, docs, lambda j, n: (fetch(j).start(), n)[1], 0)
    scale_rows[...] = scales[...].astype(f32)

    def dequantise(j, carry):
        base = pl.multiple_of(j * SPAN, SPAN)

        @pl.when(j < docs)
        def _():
            fetch(j).wait()
            position = home[ids[0, j]]
            first = (position // stored) * SCALE_ROWS + (position % stored) * 4
            cosine, sine = doc_cos[pl.ds(j, 1), :], doc_sin[pl.ds(j, 1), :]
            for b in range(SPAN // SB):
                rows = pl.ds(base + b * SB, SB)
                k = fetched[j, 0, b * SB:(b + 1) * SB, :].astype(f32) * scale_rows[pl.ds(first + b, 1), :]
                key_rows[rows, :] = rotate(k, cosine, sine)
                v = fetched[j, 1, b * SB:(b + 1) * SB, :].astype(f32) * scale_rows[pl.ds(first + 2 + b, 1), :]
                value_rows[rows, :] = v

        @pl.when(j >= docs)
        def _():
            key_rows[pl.ds(base, SPAN), :] = jnp.zeros((SPAN, HEAD), f32)
            value_rows[pl.ds(base, SPAN), :] = jnp.zeros((SPAN, HEAD), f32)

        return carry

    lax.fori_loop(0, MAXDOC, dequantise, 0)

    def patch(i, carry):
        for u in range(8):
            source = i * 8 + u
            row = recompute[source]
            key_rows[pl.ds(row, 1), :] = new_k[pl.ds(source, 1), :]
            value_rows[pl.ds(row, 1), :] = new_v[pl.ds(source, 1), :]
        return carry

    lax.fori_loop(0, recompute_total // 8, patch, 0)

    def narrow(j, carry):
        rows = pl.ds(pl.multiple_of(j * SPAN, SPAN), SPAN)
        keys[rows, :] = key_rows[rows, :].astype(bf16)
        values[rows, :] = value_rows[rows, :].astype(bf16)
        return carry

    lax.fori_loop(0, MAXDOC, narrow, 0)
    keys[context_max:context_max + SPAN, :] = new_k[recompute_total:, :].astype(bf16)
    values[context_max:context_max + SPAN, :] = new_v[recompute_total:, :].astype(bf16)
    writes = [
        pltpu.make_async_copy(keys.at[0:context_max], context.at[0], out_sem.at[0]),
        pltpu.make_async_copy(values.at[0:context_max], context.at[1], out_sem.at[1]),
    ]
    for copy in writes:
        copy.start()

    def score(g, rows):
        return lax.dot_general(q[g], keys[rows, :], (((1,), (1,)), ((), ())), preferred_element_type=f32)

    own_rows = pl.ds(context_max, SPAN)
    query_index = lax.broadcasted_iota(jnp.int32, (SPAN, SPAN), 0)
    key_index = lax.broadcasted_iota(jnp.int32, (SPAN, SPAN), 1)
    for g in range(heads):
        own = jnp.where(key_index <= query_index, score(g, own_rows), -1e30)
        scores[MAXDOC, g] = own
        top[g] = jnp.maximum(own[:, :HEAD], own[:, HEAD:])

    def first_pass(j, carry):
        rows = pl.ds(pl.multiple_of(j * SPAN, SPAN), SPAN)
        for g in range(heads):
            block = score(g, rows)
            scores[j, g] = block
            top[g] = jnp.maximum(top[g], jnp.maximum(block[:, :HEAD], block[:, HEAD:]))
        return carry

    lax.fori_loop(0, docs, first_pass, 0)
    for g in range(heads):
        top[g] = jnp.broadcast_to(jnp.max(top[g], axis=1, keepdims=True), (SPAN, HEAD))
        total[g] = jnp.zeros((SPAN, HEAD), f32)
        mixed[g] = jnp.zeros((SPAN, HEAD), f32)

    def weigh(slot, rows):
        for g in range(heads):
            peak = top[g]
            low = jnp.exp((scores[slot, g, :, :HEAD] - peak) * HEAD ** (-0.5))
            high = jnp.exp((scores[slot, g, :, HEAD:] - peak) * HEAD ** (-0.5))
            total[g] += low + high
            weights = jnp.concatenate([low.astype(bf16), high.astype(bf16)], axis=1)
            mixed[g] += jnp.dot(weights, values[rows, :], preferred_element_type=f32)

    def second_pass(j, carry):
        weigh(j, pl.ds(pl.multiple_of(j * SPAN, SPAN), SPAN))
        return carry

    lax.fori_loop(0, docs, second_pass, 0)
    weigh(MAXDOC, own_rows)
    live = lax.broadcasted_iota(jnp.int32, (SPAN, HEAD), 0) < query_len[0]
    for g in range(heads):
        result = mixed[g] / jnp.sum(total[g], axis=1, keepdims=True)
        out[:, g * HEAD:(g + 1) * HEAD] = jnp.where(live, result, 0.0).astype(bf16)
    for copy in writes:
        copy.wait()


def attend(stored, home, ids, count, recompute, query_len, codes, scales, q, new_k, new_v):
    context_max = MAXDOC * SPAN
    heads = q.shape[0]
    freq = inverse_freq()
    angle = ((np.arange(24) * SPAN).astype(np.float32)[:, None] * freq[None, :]).astype(np.float64)
    sign = np.where(np.arange(HEAD) < HALF, -1.0, 1.0)
    doc_cos = np.cos(angle).astype(np.float32)
    doc_sin = (np.sin(angle) * sign).astype(np.float32)
    return pl.pallas_call(
        functools.partial(attend_kernel, stored),
        out_shape=(
            jax.ShapeDtypeStruct((SPAN, heads * HEAD), bf16),
            jax.ShapeDtypeStruct((2, context_max, HEAD), bf16),
        ),
        in_specs=[SMEM] * 5 + [ANY] + [VMEM] * 6,
        out_specs=(VMEM, ANY),
        scratch_shapes=[
            pltpu.VMEM((MAXDOC, 2, SPAN, HEAD), bf16),
            pltpu.VMEM(scales.shape, f32),
            pltpu.VMEM((context_max, HEAD), f32),
            pltpu.VMEM((context_max, HEAD), f32),
            pltpu.VMEM((context_max + SPAN, HEAD), bf16),
            pltpu.VMEM((context_max + SPAN, HEAD), bf16),
            pltpu.VMEM((MAXDOC + 1, heads, SPAN, SPAN), f32),
            pltpu.VMEM((heads, SPAN, HEAD), f32),
            pltpu.VMEM((heads, SPAN, HEAD), f32),
            pltpu.VMEM((heads, SPAN, HEAD), f32),
            pltpu.SemaphoreType.DMA((MAXDOC,)),
            pltpu.SemaphoreType.DMA((2,)),
        ],
        compiler_params=pltpu.CompilerParams(vmem_limit_bytes=48 * 2**20),
        name="patch_attend",
    )(home, ids, count, recompute, query_len, codes, scales, doc_cos, doc_sin, q, new_k, new_v)


def on_device(
    kv_store, kv_scale, span_home, doc_ids, doc_count, recompute_rows, query_len, hidden, norm_gain, w_q, w_kv,
):
    peers, tp = lax.axis_size("store"), lax.axis_size("tp")
    stored = kv_store.shape[0]
    scales = jnp.broadcast_to(kv_scale.reshape(stored * 4, 1), (stored * 4, HEAD))
    scales = jnp.pad(scales, ((0, SCALE_ROWS - stored * 4), (0, 0)))
    flat = recompute_rows.reshape(-1)
    row_pos = jnp.concatenate([flat, doc_count[0] * SPAN + jnp.arange(SPAN, dtype=jnp.int32)])
    angles = row_pos.astype(f32)[:, None] * inverse_freq()[None, :]
    gain = norm_gain.astype(f32).reshape(1, -1)
    pairs = w_kv.reshape(-1, HEAD)
    if (peers, tp) == (8, 4):
        gathered = gather_and_project(peers, tp, hidden[0], kv_store, scales, w_q, pairs, gain, angles)
    else:
        gathered = plain_gather_and_project(hidden[0], kv_store, scales, w_q, pairs, gain, angles)
    q, new_k, new_v, codes, all_scales = gathered
    attention, context = attend(
        stored, span_home, doc_ids, doc_count, flat, query_len,
        codes.reshape((peers * stored,) + kv_store.shape[1:]), all_scales.reshape(-1, HEAD), q, new_k, new_v,
    )
    return attention[None], context[None]


def solution(mesh):
    placed = (
        P("store", None, None, "tp"),
        P("store", None, "tp", None),
        P(),
        P("store", None),
        P("store"),
        P("store", None, None),
        P("store"),
        P("store", None, "tp"),
        P(),
        P(None, "tp"),
        P(None, None, "tp"),
    )
    return jax.shard_map(
        on_device,
        mesh=mesh,
        in_specs=placed,
        out_specs=(P("store", None, "tp"), P("store", None, None, "tp")),
        check_vma=False,
    )
```

```python
import functools

import jax
import jax.numpy as jnp
import numpy as np
from jax import lax
from jax.experimental import pallas as pl
from jax.experimental.pallas import tpu as pltpu
from jax.sharding import PartitionSpec as P

SPAN = 256
SB = 128
MAXDOC = 20
HEAD = 128
HALF = HEAD // 2
CHUNK = 128
SCALE_ROWS = 16
rope_base = 500000.0
norm_eps = 1e-05
MASKED = -1e30
LOG2E = 1.4426950408889634
f32, bf16 = jnp.float32, jnp.bfloat16
MESH = pl.DeviceIdType.MESH
ANY = pl.BlockSpec(memory_space=pl.ANY)
VMEM = pl.BlockSpec(memory_space=pltpu.VMEM)
SMEM = pl.BlockSpec(memory_space=pltpu.SMEM)


def inverse_freq():
    half = np.power(rope_base, -np.arange(HALF) * (2.0 / HEAD)).astype(np.float32)
    return np.concatenate([half, half])


def rotate(values, cosine, signed_sine):
    return values * cosine + pltpu.roll(values, HALF, 1) * signed_sine


def doc_tables(rows):
    angle = ((np.arange(rows) * SPAN).astype(np.float32)[:, None] * inverse_freq()[None, :]).astype(np.float64)
    sign = np.where(np.arange(HEAD) < HALF, -1.0, 1.0)
    return np.cos(angle).astype(np.float32), (np.sin(angle) * sign).astype(np.float32)


def stream_kernel(
    home, ids, count, query_len, hidden, codes, scales, w_q, w_kv, gain, recompute, freq, doc_cos, doc_sin,
    attn_out, k_out, v_out, cached_out,
    hid, wq, wkv_raw, wkv, wide, codes_all, scales_own, scales_all, cached, queries, scores, top, total, mixed, hidden_rows,
    local_sem, cached_sem, hid_send, hid_recv, up_send, down_send, x_send, z_recv, x_recv,
):
    s = lax.axis_index("store")
    t = lax.axis_index("tp")
    z, x = s // 2, s % 2
    y, c = t // 2, t % 2
    last = 3
    across = (1 - y) * 2 + c
    sibling = y * 2 + (1 - c)
    diagonal = (1 - y) * 2 + (1 - c)
    x_peer = z * 2 + (1 - x)

    barrier = pltpu.get_barrier_semaphore()

    def greet(axis, index):
        pl.semaphore_signal(barrier, inc=1, device_id={axis: index}, device_id_type=MESH)

    greet("tp", across)
    greet("tp", sibling)
    greet("store", x_peer)
    pl.when(z > 0)(lambda: greet("store", s - 2))
    pl.when(z < last)(lambda: greet("store", s + 2))

    local = [
        pltpu.make_async_copy(w_kv, wkv_raw, local_sem.at[0]),
        pltpu.make_async_copy(w_q, wq, local_sem.at[1]),
        pltpu.make_async_copy(hidden, hid.at[t], local_sem.at[2]),
        pltpu.make_async_copy(codes, codes_all.at[s], local_sem.at[3]),
    ]

    def start_all(copies):
        for copy in copies:
            copy.start()

    start_all(local)
    stored, blocks = codes.shape[0], SPAN // SB
    scales_own[...] = jnp.zeros(scales_own.shape, f32)
    for i in range(stored):
        for part in range(2):
            pair = scales[i, part].astype(f32)
            for b in range(blocks):
                row = (i * 2 + part) * blocks + b
                scales_own[row:row + 1, :] = jnp.broadcast_to(pair[:, b:b + 1], (1, HEAD))
    pl.semaphore_wait(barrier, 3 + jnp.where(z > 0, 1, 0) + jnp.where(z < last, 1, 0))

    def span_copies(own, owner_z, column, send, recv, target):
        slot = owner_z * 2 + column
        pairs = ((codes if own else codes_all.at[slot], codes_all.at[slot], 0),
                 (scales_own if own else scales_all.at[slot], scales_all.at[slot], 1))
        return [
            pltpu.make_async_remote_copy(
                src_ref=src, dst_ref=dst, send_sem=send.at[owner_z, i], recv_sem=recv.at[owner_z, i],
                device_id={"store": target}, device_id_type=MESH,
            )
            for src, dst, i in pairs
        ]

    def up(own, owner_z):
        return span_copies(own, owner_z, x, up_send, z_recv, s + 2)

    def down(own, owner_z):
        return span_copies(own, owner_z, x, down_send, z_recv, s - 2)

    def over(own, owner_z):
        return span_copies(own, owner_z, x, x_send, x_recv, x_peer)

    def hidden_copy(kind, chunk):
        rows = pl.ds(chunk * CHUNK, CHUNK)
        slot = across if kind == 2 else t
        return pltpu.make_async_remote_copy(
            src_ref=hid.at[slot, rows] if kind == 2 else hidden.at[rows],
            dst_ref=hid.at[slot, rows],
            send_sem=hid_send.at[kind, chunk], recv_sem=hid_recv.at[kind, chunk],
            device_id={"tp": across if kind == 0 else sibling}, device_id_type=MESH,
        )

    def hidden_arrival(kind, chunk):
        rows = pl.ds(chunk * CHUNK, CHUNK)
        slot = (across, sibling, diagonal)[kind]
        pltpu.make_async_remote_copy(
            src_ref=hidden.at[rows], dst_ref=hid.at[slot, rows],
            send_sem=hid_send.at[kind, chunk], recv_sem=hid_recv.at[kind, chunk],
            device_id={"tp": across if kind == 0 else sibling}, device_id_type=MESH,
        ).wait_recv()

    chunks = hidden.shape[0] // CHUNK
    query_chunks = SPAN // CHUNK
    first_query = chunks - query_chunks
    order = list(range(first_query, chunks)) + list(range(first_query))

    start_all(over(True, z))
    pl.when(z < last)(lambda: start_all(up(True, z)))
    pl.when(z > 0)(lambda: start_all(down(True, z)))
    for chunk in order:
        hidden_copy(0, chunk).start()
    for chunk in order:
        hidden_copy(1, chunk).start()

    docs = count[0]
    positions = [home[ids[0, j]] for j in range(MAXDOC)]
    table_rows = hidden_rows.shape[0]
    hits = jnp.zeros((table_rows, SPAN), f32)
    for r in range(recompute.shape[0]):
        row = recompute[r:r + 1, :]
        doc_match = lax.broadcasted_iota(jnp.int32, (table_rows, CHUNK), 0) == (row >> 8)
        row_match = lax.broadcasted_iota(jnp.int32, (SPAN, CHUNK), 0) == (row & 255)
        hits = hits + lax.dot_general(
            jnp.where(doc_match, 1.0, 0.0).astype(bf16), jnp.where(row_match, 1.0, 0.0).astype(bf16),
            (((1,), (1,)), ((), ())), preferred_element_type=f32,
        )
    dead = lax.broadcasted_iota(jnp.int32, (table_rows, SPAN), 0) >= docs
    hidden_rows[...] = jnp.where(jnp.logical_or(dead, hits > 0.5), MASKED, 0.0)
    top[...] = jnp.full(top.shape, MASKED, f32)
    total[...] = jnp.zeros(total.shape, f32)
    mixed[...] = jnp.zeros(mixed.shape, f32)

    local[0].wait()
    block = wide.shape[0]

    def split_pairs(i, carry):
        wide[...] = wkv_raw[pl.ds(pl.multiple_of(i * block, block), block), :].astype(f32)
        rows = pl.ds(pl.multiple_of(i * (block // 2), block // 2), block // 2)
        wkv[rows, 0:HEAD] = wide[pl.ds(0, block // 2, stride=2), :].astype(bf16)
        wkv[rows, HEAD:2 * HEAD] = wide[pl.ds(1, block // 2, stride=2), :].astype(bf16)
        return carry

    lax.fori_loop(0, wkv_raw.shape[0] // block, split_pairs, 0)
    for copy in local[1:]:
        copy.wait()

    parts, _, width = hid.shape
    heads = wq.shape[1] // HEAD
    own_slot = cached.shape[0] - 1

    def row_angles(chunk):
        if chunk >= first_query:
            offset = docs * SPAN + (chunk - first_query) * CHUNK
            place = lax.broadcasted_iota(jnp.int32, (CHUNK, HEAD), 0) + offset
            return place.astype(f32) * freq[...]
        row = jnp.broadcast_to(recompute[chunk:chunk + 1, :].astype(f32), (CHUNK, CHUNK))
        down_rows = lax.broadcasted_iota(jnp.int32, (CHUNK, CHUNK), 0)
        diagonal_entry = down_rows == lax.broadcasted_iota(jnp.int32, (CHUNK, CHUNK), 1)
        return jnp.sum(jnp.where(diagonal_entry, row, 0.0), axis=1, keepdims=True) * freq[...]

    def project(chunk):
        hidden_arrival(1, chunk)
        hidden_arrival(2, chunk)
        rows = pl.ds(chunk * CHUNK, CHUNK)
        squares = jnp.zeros((CHUNK, 1), f32)
        for part in range(parts):
            values = hid[part, rows, :].astype(f32)
            squares = squares + jnp.sum(values * values, axis=1, keepdims=True)
        inverse_rms = lax.rsqrt(squares * (1.0 / (parts * width)) + norm_eps)
        kv = jnp.zeros((CHUNK, 2 * HEAD), f32)
        is_query = chunk >= first_query
        q = jnp.zeros((CHUNK, wq.shape[1]), f32)
        for part in range(parts):
            columns = pl.ds(part * width, width)
            normed = (hid[part, rows, :].astype(f32) * inverse_rms * gain[:, columns]).astype(bf16)
            kv = kv + jnp.dot(normed, wkv[columns, :], preferred_element_type=f32)
            if is_query:
                q = q + jnp.dot(normed, wq[columns, :], preferred_element_type=f32)
        angle = row_angles(chunk)
        cosine, sine = jnp.cos(angle), jnp.sin(angle)
        sine = jnp.where(lax.broadcasted_iota(jnp.int32, angle.shape, 1) < HALF, -sine, sine)
        new_key = rotate(kv[:, :HEAD], cosine, sine)
        per_span = SPAN // CHUNK
        place = pl.ds(chunk % per_span * CHUNK, CHUNK)
        cached[own_slot, chunk // per_span, 0, place, :] = new_key.astype(bf16)
        cached[own_slot, chunk // per_span, 1, place, :] = kv[:, HEAD:].astype(bf16)
        if is_query:
            for g in range(heads):
                q_rows = pl.ds(g * SPAN + (chunk - first_query) * CHUNK, CHUNK)
                queries[q_rows, :] = rotate(q[:, g * HEAD:(g + 1) * HEAD], cosine, sine).astype(bf16)
        else:
            k_out[rows, :] = new_key
            v_out[rows, :] = kv[:, HEAD:]

    exponent = HEAD ** (-0.5) * LOG2E
    query_block = scores.shape[1]

    def attend_group(slot, bias, causal):
        def some_queries(n, carry):
            rows = pl.ds(pl.multiple_of(n * query_block, query_block), query_block)
            q = queries[rows, :]
            before = top[rows, :]
            peak = before
            for i in range(stored):
                part = lax.dot_general(
                    q, cached[slot, i, 0], (((1,), (1,)), ((), ())), preferred_element_type=f32
                )
                if bias is not None:
                    part = part + bias[i]
                elif causal and i == stored - 1:
                    query_index = lax.broadcasted_iota(jnp.int32, (query_block, SPAN), 0) & (SPAN - 1)
                    key_index = lax.broadcasted_iota(jnp.int32, (query_block, SPAN), 1)
                    part = jnp.where(key_index <= query_index, part, MASKED)
                scores[i] = part
                peak = jnp.maximum(peak, jnp.maximum(part[:, :HEAD], part[:, HEAD:]))
            peak = jnp.broadcast_to(jnp.max(peak, axis=1, keepdims=True), (query_block, HEAD))
            top[rows, :] = peak
            fade = jnp.exp2((before - peak) * exponent)
            sums = total[rows, :] * fade
            gained = jnp.zeros((query_block, HEAD), f32)
            for i in range(stored):
                low = jnp.exp2((scores[i, :, :HEAD] - peak) * exponent)
                high = jnp.exp2((scores[i, :, HEAD:] - peak) * exponent)
                sums = sums + (low + high)
                weights = jnp.concatenate([low.astype(bf16), high.astype(bf16)], axis=1)
                gained = gained + jnp.dot(weights, cached[slot, i, 1], preferred_element_type=f32)
            total[rows, :] = sums
            mixed[rows, :] = mixed[rows, :] * fade + gained
            return carry

        lax.fori_loop(0, queries.shape[0] // query_block, some_queries, 0)

    def keep_cached(slot):
        return pltpu.make_async_copy(cached.at[slot], cached_out.at[slot], cached_sem.at[slot])

    def span_group(slot):
        bias = []
        for i in range(stored):
            position = slot * stored + i
            doc = table_rows - 1
            for j in range(MAXDOC):
                doc = doc + jnp.where(positions[j] == position, j - (table_rows - 1), 0)
            doc = jnp.clip(doc, 0, table_rows - 1)
            cosine, sine = doc_cos[pl.ds(doc, 1), :], doc_sin[pl.ds(doc, 1), :]
            bias.append(hidden_rows[pl.ds(doc, 1), :])
            for b in range(blocks):
                rows = slice(b * SB, (b + 1) * SB)
                first = i * 2 * blocks + b
                k = codes_all[slot, i, 0, rows, :].astype(f32) * scales_all[slot, first:first + 1, :]
                cached[slot, i, 0, rows, :] = rotate(k, cosine, sine).astype(bf16)
                first = first + blocks
                v = codes_all[slot, i, 1, rows, :].astype(f32) * scales_all[slot, first:first + 1, :]
                cached[slot, i, 1, rows, :] = v.astype(bf16)
        keep_cached(slot).start()
        attend_group(slot, bias, False)

    def span_step(k):
        @pl.when(z >= k)
        def _():
            for copy in up(False, z - k):
                copy.wait_recv()
            start_all(over(False, z - k))
            pl.when(z < last)(lambda: start_all(up(False, z - k)))

        @pl.when(z + k <= last)
        def _():
            for copy in down(False, z + k):
                copy.wait_recv()
            start_all(over(False, z + k))
            pl.when(z > 0)(lambda: start_all(down(False, z + k)))

    folded = jnp.where(z < 2, z, last - z)

    def near(k):
        owner = jnp.where(folded == 0, k, (1, 0, 2, 3)[k])
        return jnp.where(z < 2, owner, last - owner)

    def same_column(k):
        span_group(near(k) * 2 + x)

    def other_column(k):
        for copy in span_copies(False, near(k), 1 - x, x_send, x_recv, x_peer):
            copy.wait_recv()
        span_group(near(k) * 2 + 1 - x)

    def relay(i):
        hidden_arrival(0, order[i])
        hidden_copy(2, order[i]).start()

    relay(0)
    scales_all[s] = scales_own[...]
    project(order[0])
    span_step(1)
    relay(1)
    project(order[1])
    same_column(0)
    relay(2)
    span_step(2)
    other_column(0)
    project(order[2])
    same_column(1)
    relay(3)
    span_step(3)
    other_column(1)
    project(order[3])
    relay(4)
    same_column(2)
    same_column(3)
    project(order[4])
    other_column(2)
    relay(5)
    project(order[5])
    attend_group(own_slot, None, True)
    other_column(3)

    live = lax.broadcasted_iota(jnp.int32, (SPAN, HEAD), 0) < query_len[0]
    for g in range(heads):
        rows = pl.ds(g * SPAN, SPAN)
        result = mixed[rows, :] / jnp.sum(total[rows, :], axis=1, keepdims=True)
        attn_out[:, g * HEAD:(g + 1) * HEAD] = jnp.where(live, result, 0.0).astype(bf16)

    for slot in range(own_slot):
        keep_cached(slot).wait()
    for chunk in range(chunks):
        for kind in range(3):
            hidden_copy(kind, chunk).wait_send()
    for owner in range(4):
        for copy in over(False, owner):
            copy.wait_send()

        @pl.when(jnp.logical_and(z < last, owner <= z))
        def _():
            for copy in up(False, owner):
                copy.wait_send()

        @pl.when(jnp.logical_and(z > 0, owner >= z))
        def _():
            for copy in down(False, owner):
                copy.wait_send()


def stream(peers, tp, home, ids, count, query_len, hidden, codes, scales, w_q, w_kv, gain, recompute):
    rows, width = hidden.shape
    features = w_q.shape[0]
    heads = w_q.shape[1] // HEAD
    chunks = rows // CHUNK
    table_rows = 32
    doc_cos, doc_sin = doc_tables(table_rows)
    fresh = rows - SPAN
    dma = pltpu.SemaphoreType.DMA
    return pl.pallas_call(
        stream_kernel,
        out_shape=(
            jax.ShapeDtypeStruct((SPAN, heads * HEAD), bf16),
            jax.ShapeDtypeStruct((fresh, HEAD), f32),
            jax.ShapeDtypeStruct((fresh, HEAD), f32),
            jax.ShapeDtypeStruct((peers,) + codes.shape, bf16),
        ),
        in_specs=[SMEM] * 4 + [ANY, ANY, VMEM, ANY, ANY] + [VMEM] * 5,
        out_specs=(VMEM, VMEM, VMEM, ANY),
        scratch_shapes=[
            pltpu.VMEM((tp, rows, width), bf16),
            pltpu.VMEM((features, w_q.shape[1]), bf16),
            pltpu.VMEM((2 * features, HEAD), bf16),
            pltpu.VMEM((features, 2 * HEAD), bf16),
            pltpu.VMEM((512, HEAD), f32),
            pltpu.VMEM((peers,) + codes.shape, bf16),
            pltpu.VMEM((SCALE_ROWS, HEAD), f32),
            pltpu.VMEM((peers, SCALE_ROWS, HEAD), f32),
            pltpu.VMEM((peers + 1,) + codes.shape, bf16),
            pltpu.VMEM((heads * SPAN, HEAD), bf16),
            pltpu.VMEM((codes.shape[0], 2 * SPAN, SPAN), f32),
            pltpu.VMEM((heads * SPAN, HEAD), f32),
            pltpu.VMEM((heads * SPAN, HEAD), f32),
            pltpu.VMEM((heads * SPAN, HEAD), f32),
            pltpu.VMEM((table_rows, SPAN), f32),
            dma((4,)),
            dma((peers,)),
            dma((3, chunks)),
            dma((3, chunks)),
            dma((4, 2)),
            dma((4, 2)),
            dma((4, 2)),
            dma((4, 2)),
            dma((4, 2)),
        ],
        compiler_params=pltpu.CompilerParams(
            collective_id=0, has_side_effects=True, vmem_limit_bytes=60 * 2**20
        ),
        name="stream_attend",
    )(home, ids, count, query_len, hidden, codes, scales, w_q, w_kv, gain, recompute,
      inverse_freq()[None, :], doc_cos, doc_sin)


def place_kernel(
    home, ids, count, recompute, attended, cached, new_k, new_v,
    out, context,
    fetched, key_rows, value_rows, keys, values, fetch_sem, out_sem,
):
    docs = count[0]
    passed = pltpu.make_async_copy(attended, out, out_sem.at[2])
    passed.start()

    def fetch(j):
        return pltpu.make_async_copy(cached.at[home[ids[0, j]]], fetched.at[j], fetch_sem.at[j])

    lax.fori_loop(0, docs, lambda j, n: (fetch(j).start(), n)[1], 0)

    def widen(j, carry):
        rows = pl.ds(pl.multiple_of(j * SPAN, SPAN), SPAN)

        @pl.when(j < docs)
        def _():
            fetch(j).wait()
            key_rows[rows, :] = fetched[j, 0].astype(f32)
            value_rows[rows, :] = fetched[j, 1].astype(f32)

        @pl.when(j >= docs)
        def _():
            key_rows[rows, :] = jnp.zeros((SPAN, HEAD), f32)
            value_rows[rows, :] = jnp.zeros((SPAN, HEAD), f32)

        return carry

    lax.fori_loop(0, MAXDOC, widen, 0)
    step = 16

    def patch(i, carry):
        for u in range(step):
            source = i * step + u
            row = recompute[source // CHUNK, source % CHUNK]
            key_rows[pl.ds(row, 1), :] = new_k[pl.ds(source, 1), :]
            value_rows[pl.ds(row, 1), :] = new_v[pl.ds(source, 1), :]
        return carry

    lax.fori_loop(0, new_k.shape[0] // step, patch, 0)
    writes = [
        pltpu.make_async_copy(keys, context.at[0], out_sem.at[0]),
        pltpu.make_async_copy(values, context.at[1], out_sem.at[1]),
    ]
    for source, target, copy in ((key_rows, keys, writes[0]), (value_rows, values, writes[1])):
        def narrow(j, carry, source=source, target=target):
            rows = pl.ds(pl.multiple_of(j * SPAN, SPAN), SPAN)
            target[rows, :] = source[rows, :].astype(bf16)
            return carry

        lax.fori_loop(0, MAXDOC, narrow, 0)
        copy.start()
    for copy in writes:
        copy.wait()
    passed.wait()


def place(home, ids, count, recompute, attended, cached, new_k, new_v):
    context_max = MAXDOC * SPAN
    return pl.pallas_call(
        place_kernel,
        out_shape=(
            jax.ShapeDtypeStruct(attended.shape, bf16),
            jax.ShapeDtypeStruct((2, context_max, HEAD), bf16),
        ),
        in_specs=[SMEM] * 4 + [ANY, ANY, VMEM, VMEM],
        out_specs=(ANY, ANY),
        scratch_shapes=[
            pltpu.VMEM((MAXDOC, 2, SPAN, HEAD), bf16),
            pltpu.VMEM((context_max, HEAD), f32),
            pltpu.VMEM((context_max, HEAD), f32),
            pltpu.VMEM((context_max, HEAD), bf16),
            pltpu.VMEM((context_max, HEAD), bf16),
            pltpu.SemaphoreType.DMA((MAXDOC,)),
            pltpu.SemaphoreType.DMA((3,)),
        ],
        compiler_params=pltpu.CompilerParams(vmem_limit_bytes=60 * 2**20),
        name="place_context",
    )(home, ids, count, recompute, attended, cached, new_k, new_v)


def plain_gather_and_project(hidden, codes, scales, w_q, w_kv, gain, angles):
    rows = hidden.shape[0]
    heads = w_q.shape[1] // HEAD
    all_codes = lax.all_gather(codes, "store", axis=0)
    all_scales = lax.all_gather(scales, "store", axis=0)
    features = lax.all_gather(hidden, "tp", axis=1, tiled=True).astype(f32)
    inverse_rms = lax.rsqrt(jnp.mean(features * features, axis=-1, keepdims=True) + norm_eps)
    normed = (features * inverse_rms * gain).astype(bf16)
    cosine, sine = jnp.cos(angles), jnp.sin(angles)
    sine = jnp.where(jnp.arange(HEAD)[None, :] < HALF, -sine, sine)
    kv = jnp.dot(normed, w_kv.reshape(-1, 2 * HEAD), preferred_element_type=f32)
    q = jnp.dot(normed[rows - SPAN:], w_q, preferred_element_type=f32)
    q = jnp.transpose(q.reshape(SPAN, heads, HEAD), (1, 0, 2))

    def turn(values, cosine, sine):
        return values * cosine + jnp.roll(values, HALF, axis=-1) * sine

    new_keys = turn(kv[:, :HEAD], cosine, sine)
    q = turn(q, cosine[rows - SPAN:], sine[rows - SPAN:]).astype(bf16)
    return q, new_keys, kv[:, HEAD:], all_codes, all_scales


def attend_kernel(
    stored, home, ids, count, recompute, query_len, codes, scales, doc_cos, doc_sin, q, new_k, new_v,
    out, context,
    fetched, scale_rows, key_rows, value_rows, keys, values, scores, top, total, mixed, fetch_sem, out_sem,
):
    docs = count[0]
    recompute_total = recompute.shape[0]
    context_max = MAXDOC * SPAN
    heads = q.shape[0]

    def fetch(j):
        position = home[ids[0, j]]
        return pltpu.make_async_copy(codes.at[position], fetched.at[j], fetch_sem.at[j])

    lax.fori_loop(0, docs, lambda j, n: (fetch(j).start(), n)[1], 0)
    scale_rows[...] = scales[...].astype(f32)

    def dequantise(j, carry):
        base = pl.multiple_of(j * SPAN, SPAN)

        @pl.when(j < docs)
        def _():
            fetch(j).wait()
            position = home[ids[0, j]]
            first = (position // stored) * SCALE_ROWS + (position % stored) * 4
            cosine, sine = doc_cos[pl.ds(j, 1), :], doc_sin[pl.ds(j, 1), :]
            for b in range(SPAN // SB):
                rows = pl.ds(base + b * SB, SB)
                k = fetched[j, 0, b * SB:(b + 1) * SB, :].astype(f32) * scale_rows[pl.ds(first + b, 1), :]
                key_rows[rows, :] = rotate(k, cosine, sine)
                v = fetched[j, 1, b * SB:(b + 1) * SB, :].astype(f32) * scale_rows[pl.ds(first + 2 + b, 1), :]
                value_rows[rows, :] = v

        @pl.when(j >= docs)
        def _():
            key_rows[pl.ds(base, SPAN), :] = jnp.zeros((SPAN, HEAD), f32)
            value_rows[pl.ds(base, SPAN), :] = jnp.zeros((SPAN, HEAD), f32)

        return carry

    lax.fori_loop(0, MAXDOC, dequantise, 0)

    def patch(i, carry):
        for u in range(8):
            source = i * 8 + u
            row = recompute[source]
            key_rows[pl.ds(row, 1), :] = new_k[pl.ds(source, 1), :]
            value_rows[pl.ds(row, 1), :] = new_v[pl.ds(source, 1), :]
        return carry

    lax.fori_loop(0, recompute_total // 8, patch, 0)

    def narrow(j, carry):
        rows = pl.ds(pl.multiple_of(j * SPAN, SPAN), SPAN)
        keys[rows, :] = key_rows[rows, :].astype(bf16)
        values[rows, :] = value_rows[rows, :].astype(bf16)
        return carry

    lax.fori_loop(0, MAXDOC, narrow, 0)
    keys[context_max:context_max + SPAN, :] = new_k[recompute_total:, :].astype(bf16)
    values[context_max:context_max + SPAN, :] = new_v[recompute_total:, :].astype(bf16)
    writes = [
        pltpu.make_async_copy(keys.at[0:context_max], context.at[0], out_sem.at[0]),
        pltpu.make_async_copy(values.at[0:context_max], context.at[1], out_sem.at[1]),
    ]
    for copy in writes:
        copy.start()

    def score(g, rows):
        return lax.dot_general(q[g], keys[rows, :], (((1,), (1,)), ((), ())), preferred_element_type=f32)

    own_rows = pl.ds(context_max, SPAN)
    query_index = lax.broadcasted_iota(jnp.int32, (SPAN, SPAN), 0)
    key_index = lax.broadcasted_iota(jnp.int32, (SPAN, SPAN), 1)
    for g in range(heads):
        own = jnp.where(key_index <= query_index, score(g, own_rows), -1e30)
        scores[MAXDOC, g] = own
        top[g] = jnp.maximum(own[:, :HEAD], own[:, HEAD:])

    def first_pass(j, carry):
        rows = pl.ds(pl.multiple_of(j * SPAN, SPAN), SPAN)
        for g in range(heads):
            block = score(g, rows)
            scores[j, g] = block
            top[g] = jnp.maximum(top[g], jnp.maximum(block[:, :HEAD], block[:, HEAD:]))
        return carry

    lax.fori_loop(0, docs, first_pass, 0)
    for g in range(heads):
        top[g] = jnp.broadcast_to(jnp.max(top[g], axis=1, keepdims=True), (SPAN, HEAD))
        total[g] = jnp.zeros((SPAN, HEAD), f32)
        mixed[g] = jnp.zeros((SPAN, HEAD), f32)

    def weigh(slot, rows):
        for g in range(heads):
            peak = top[g]
            low = jnp.exp((scores[slot, g, :, :HEAD] - peak) * HEAD ** (-0.5))
            high = jnp.exp((scores[slot, g, :, HEAD:] - peak) * HEAD ** (-0.5))
            total[g] += low + high
            weights = jnp.concatenate([low.astype(bf16), high.astype(bf16)], axis=1)
            mixed[g] += jnp.dot(weights, values[rows, :], preferred_element_type=f32)

    def second_pass(j, carry):
        weigh(j, pl.ds(pl.multiple_of(j * SPAN, SPAN), SPAN))
        return carry

    lax.fori_loop(0, docs, second_pass, 0)
    weigh(MAXDOC, own_rows)
    live = lax.broadcasted_iota(jnp.int32, (SPAN, HEAD), 0) < query_len[0]
    for g in range(heads):
        result = mixed[g] / jnp.sum(total[g], axis=1, keepdims=True)
        out[:, g * HEAD:(g + 1) * HEAD] = jnp.where(live, result, 0.0).astype(bf16)
    for copy in writes:
        copy.wait()


def attend(stored, home, ids, count, recompute, query_len, codes, scales, q, new_k, new_v):
    context_max = MAXDOC * SPAN
    heads = q.shape[0]
    freq = inverse_freq()
    angle = ((np.arange(24) * SPAN).astype(np.float32)[:, None] * freq[None, :]).astype(np.float64)
    sign = np.where(np.arange(HEAD) < HALF, -1.0, 1.0)
    doc_cos = np.cos(angle).astype(np.float32)
    doc_sin = (np.sin(angle) * sign).astype(np.float32)
    return pl.pallas_call(
        functools.partial(attend_kernel, stored),
        out_shape=(
            jax.ShapeDtypeStruct((SPAN, heads * HEAD), bf16),
            jax.ShapeDtypeStruct((2, context_max, HEAD), bf16),
        ),
        in_specs=[SMEM] * 5 + [ANY] + [VMEM] * 6,
        out_specs=(VMEM, ANY),
        scratch_shapes=[
            pltpu.VMEM((MAXDOC, 2, SPAN, HEAD), bf16),
            pltpu.VMEM(scales.shape, f32),
            pltpu.VMEM((context_max, HEAD), f32),
            pltpu.VMEM((context_max, HEAD), f32),
            pltpu.VMEM((context_max + SPAN, HEAD), bf16),
            pltpu.VMEM((context_max + SPAN, HEAD), bf16),
            pltpu.VMEM((MAXDOC + 1, heads, SPAN, SPAN), f32),
            pltpu.VMEM((heads, SPAN, HEAD), f32),
            pltpu.VMEM((heads, SPAN, HEAD), f32),
            pltpu.VMEM((heads, SPAN, HEAD), f32),
            pltpu.SemaphoreType.DMA((MAXDOC,)),
            pltpu.SemaphoreType.DMA((2,)),
        ],
        compiler_params=pltpu.CompilerParams(vmem_limit_bytes=48 * 2**20),
        name="patch_attend",
    )(home, ids, count, recompute, query_len, codes, scales, doc_cos, doc_sin, q, new_k, new_v)


def on_device(
    kv_store, kv_scale, span_home, doc_ids, doc_count, recompute_rows, query_len, hidden, norm_gain, w_q, w_kv,
):
    peers, tp = lax.axis_size("store"), lax.axis_size("tp")
    stored = kv_store.shape[0]
    gain = norm_gain.astype(f32).reshape(1, -1)
    pairs = w_kv.reshape(-1, HEAD)
    if (peers, tp) == (8, 4):
        attended, new_k, new_v, cached = stream(
            peers, tp, span_home, doc_ids, doc_count, query_len, hidden[0], kv_store, kv_scale, w_q, pairs, gain,
            recompute_rows[0],
        )
        cached = cached.reshape((peers * stored,) + kv_store.shape[1:])
        attention, context = place(
            span_home, doc_ids, doc_count, recompute_rows[0], attended, cached, new_k, new_v
        )
        return attention[None], context[None]
    scales = jnp.broadcast_to(kv_scale.reshape(stored * 4, 1), (stored * 4, HEAD))
    scales = jnp.pad(scales, ((0, SCALE_ROWS - stored * 4), (0, 0)))
    flat = recompute_rows.reshape(-1)
    row_pos = jnp.concatenate([flat, doc_count[0] * SPAN + jnp.arange(SPAN, dtype=jnp.int32)])
    angles = row_pos.astype(f32)[:, None] * inverse_freq()[None, :]
    gathered = plain_gather_and_project(hidden[0], kv_store, scales, w_q, pairs, gain, angles)
    q, new_k, new_v, codes, all_scales = gathered
    attention, context = attend(
        stored, span_home, doc_ids, doc_count, flat, query_len,
        codes.reshape((peers * stored,) + kv_store.shape[1:]), all_scales.reshape(-1, HEAD), q, new_k, new_v,
    )
    return attention[None], context[None]


def solution(mesh):
    placed = (
        P("store", None, None, "tp"),
        P("store", None, "tp", None),
        P(),
        P("store", None),
        P("store"),
        P("store", None, None),
        P("store"),
        P("store", None, "tp"),
        P(),
        P(None, "tp"),
        P(None, None, "tp"),
    )
    return jax.shard_map(
        on_device,
        mesh=mesh,
        in_specs=placed,
        out_specs=(P("store", None, "tp"), P("store", None, None, "tp")),
        check_vma=False,
    )
```

```python
import functools

import jax
import jax.numpy as jnp
import numpy as np
from jax import lax
from jax.experimental import pallas as pl
from jax.experimental.pallas import tpu as pltpu
from jax.sharding import PartitionSpec as P

SPAN = 256
SB = 128
MAXDOC = 20
HEAD = 128
HALF = HEAD // 2
CHUNK = 128
SCALE_ROWS = 16
rope_base = 500000.0
norm_eps = 1e-05
MASKED = -1e30
LOG2E = 1.4426950408889634
NORM_ROWS = 16
TILE = 32
f32, bf16 = jnp.float32, jnp.bfloat16
MESH = pl.DeviceIdType.MESH
ANY = pl.BlockSpec(memory_space=pl.ANY)
VMEM = pl.BlockSpec(memory_space=pltpu.VMEM)
SMEM = pl.BlockSpec(memory_space=pltpu.SMEM)


def inverse_freq():
    half = np.power(rope_base, -np.arange(HALF) * (2.0 / HEAD)).astype(np.float32)
    return np.concatenate([half, half])


def rotate(values, cosine, signed_sine):
    return values * cosine + pltpu.roll(values, HALF, 1) * signed_sine


def doc_tables(rows):
    angle = ((np.arange(rows) * SPAN).astype(np.float32)[:, None] * inverse_freq()[None, :]).astype(np.float64)
    sign = np.where(np.arange(HEAD) < HALF, -1.0, 1.0)
    return np.cos(angle).astype(np.float32), (np.sin(angle) * sign).astype(np.float32)


def stream_kernel(
    home, ids, count, query_len, hidden, codes, scales, w_q, w_kv, gain, recompute, freq, doc_cos, doc_sin,
    attn_out, fresh_out, cached_out,
    hid, wq, wkv_raw, wkv, wide, codes_all, scales_own, scales_all, cached, queries, scores, weights, normed, gains,
    top, total, mixed, hidden_rows,
    local_sem, cached_sem, hid_send, hid_recv, up_send, down_send, x_send, z_recv, x_recv,
):
    s = lax.axis_index("store")
    t = lax.axis_index("tp")
    z, x = s // 2, s % 2
    y, c = t // 2, t % 2
    last = 3
    across = (1 - y) * 2 + c
    sibling = y * 2 + (1 - c)
    diagonal = (1 - y) * 2 + (1 - c)
    x_peer = z * 2 + (1 - x)

    barrier = pltpu.get_barrier_semaphore()

    def greet(axis, index):
        pl.semaphore_signal(barrier, inc=1, device_id={axis: index}, device_id_type=MESH)

    greet("tp", across)
    greet("tp", sibling)
    greet("store", x_peer)
    pl.when(z > 0)(lambda: greet("store", s - 2))
    pl.when(z < last)(lambda: greet("store", s + 2))

    local = [
        pltpu.make_async_copy(w_kv, wkv_raw, local_sem.at[0]),
        pltpu.make_async_copy(w_q, wq, local_sem.at[1]),
        pltpu.make_async_copy(hidden, hid.at[t], local_sem.at[2]),
        pltpu.make_async_copy(codes, codes_all.at[s], local_sem.at[3]),
    ]

    def start_all(copies):
        for copy in copies:
            copy.start()

    start_all(local)
    stored, blocks = codes.shape[0], SPAN // SB
    scales_own[...] = jnp.zeros(scales_own.shape, f32)
    for i in range(stored):
        for part in range(2):
            pair = scales[0, part].astype(f32)
            for b in range(blocks):
                row = (i * 2 + part) * blocks + b
                scales_own[row:row + 1, :] = jnp.broadcast_to(pair[b:b + 1, i:i + 1], (1, HEAD))
    pl.semaphore_wait(barrier, 3 + jnp.where(z > 0, 1, 0) + jnp.where(z < last, 1, 0))

    def span_copies(own, owner_z, column, send, recv, target):
        slot = owner_z * 2 + column
        pairs = ((codes if own else codes_all.at[slot], codes_all.at[slot], 0),
                 (scales_own if own else scales_all.at[slot], scales_all.at[slot], 1))
        return [
            pltpu.make_async_remote_copy(
                src_ref=src, dst_ref=dst, send_sem=send.at[owner_z, i], recv_sem=recv.at[owner_z, i],
                device_id={"store": target}, device_id_type=MESH,
            )
            for src, dst, i in pairs
        ]

    def up(own, owner_z):
        return span_copies(own, owner_z, x, up_send, z_recv, s + 2)

    def down(own, owner_z):
        return span_copies(own, owner_z, x, down_send, z_recv, s - 2)

    def over(own, owner_z):
        return span_copies(own, owner_z, x, x_send, x_recv, x_peer)

    def hidden_copy(kind, chunk):
        rows = pl.ds(chunk * CHUNK, CHUNK)
        slot = across if kind == 2 else t
        return pltpu.make_async_remote_copy(
            src_ref=hid.at[slot, rows] if kind == 2 else hidden.at[rows],
            dst_ref=hid.at[slot, rows],
            send_sem=hid_send.at[kind, chunk], recv_sem=hid_recv.at[kind, chunk],
            device_id={"tp": across if kind == 0 else sibling}, device_id_type=MESH,
        )

    def hidden_arrival(kind, chunk):
        rows = pl.ds(chunk * CHUNK, CHUNK)
        slot = (across, sibling, diagonal)[kind]
        pltpu.make_async_remote_copy(
            src_ref=hidden.at[rows], dst_ref=hid.at[slot, rows],
            send_sem=hid_send.at[kind, chunk], recv_sem=hid_recv.at[kind, chunk],
            device_id={"tp": across if kind == 0 else sibling}, device_id_type=MESH,
        ).wait_recv()

    chunks = hidden.shape[0] // CHUNK
    query_chunks = SPAN // CHUNK
    first_query = chunks - query_chunks
    order = list(range(first_query, chunks)) + list(range(first_query))

    start_all(over(True, z))
    pl.when(z < last)(lambda: start_all(up(True, z)))
    pl.when(z > 0)(lambda: start_all(down(True, z)))
    for chunk in order:
        hidden_copy(0, chunk).start()
    for chunk in order:
        hidden_copy(1, chunk).start()

    gains[...] = gain[...].astype(f32).reshape(gains.shape)
    docs = count[0]
    positions = [home[ids[0, j]] for j in range(MAXDOC)]
    table_rows = hidden_rows.shape[0]
    hits = jnp.zeros((table_rows, SPAN), f32)
    for r in range(recompute.shape[0]):
        row = recompute[r:r + 1, :]
        doc_match = lax.broadcasted_iota(jnp.int32, (table_rows, CHUNK), 0) == (row >> 8)
        row_match = lax.broadcasted_iota(jnp.int32, (SPAN, CHUNK), 0) == (row & 255)
        hits = hits + lax.dot_general(
            jnp.where(doc_match, 1.0, 0.0).astype(bf16), jnp.where(row_match, 1.0, 0.0).astype(bf16),
            (((1,), (1,)), ((), ())), preferred_element_type=f32,
        )
    dead = lax.broadcasted_iota(jnp.int32, (table_rows, SPAN), 0) >= docs
    hidden_rows[...] = jnp.where(jnp.logical_or(dead, hits > 0.5), MASKED, 0.0)
    top[...] = jnp.full(top.shape, MASKED, f32)
    total[...] = jnp.zeros(total.shape, f32)
    mixed[...] = jnp.zeros(mixed.shape, f32)

    local[0].wait()
    block = wide.shape[0]

    def split_pairs(i, carry):
        wide[...] = wkv_raw[pl.ds(pl.multiple_of(i * block, block), block), :].astype(f32)
        rows = pl.ds(pl.multiple_of(i * (block // 2), block // 2), block // 2)
        wkv[rows, 0:HEAD] = wide[pl.ds(0, block // 2, stride=2), :].astype(bf16)
        wkv[rows, HEAD:2 * HEAD] = wide[pl.ds(1, block // 2, stride=2), :].astype(bf16)
        return carry

    lax.fori_loop(0, wkv_raw.shape[0] // block, split_pairs, 0)
    for copy in local[1:]:
        copy.wait()

    parts, _, width = hid.shape
    heads = wq.shape[1] // HEAD
    own_slot = cached.shape[0] - 1

    def row_angles(chunk):
        if chunk >= first_query:
            offset = docs * SPAN + (chunk - first_query) * CHUNK
            place = lax.broadcasted_iota(jnp.int32, (CHUNK, HEAD), 0) + offset
            return place.astype(f32) * freq[...]
        row = jnp.broadcast_to(recompute[chunk:chunk + 1, :].astype(f32), (CHUNK, CHUNK))
        down_rows = lax.broadcasted_iota(jnp.int32, (CHUNK, CHUNK), 0)
        diagonal_entry = down_rows == lax.broadcasted_iota(jnp.int32, (CHUNK, CHUNK), 1)
        return jnp.sum(jnp.where(diagonal_entry, row, 0.0), axis=1, keepdims=True) * freq[...]

    def normalise(chunk, place):
        hidden_arrival(1, chunk)
        hidden_arrival(2, chunk)

        def some_rows(i, carry):
            rows = pl.ds(pl.multiple_of(chunk * CHUNK + i * NORM_ROWS, NORM_ROWS), NORM_ROWS)
            placed = pl.ds(pl.multiple_of(place * CHUNK + i * NORM_ROWS, NORM_ROWS), NORM_ROWS)
            squares = jnp.zeros((NORM_ROWS, HEAD), f32)
            for part in range(parts):
                for block in range(width // HEAD):
                    value = hid[part, rows, block * HEAD:(block + 1) * HEAD].astype(f32)
                    squares = squares + value * value
            mean = jnp.sum(squares, axis=1, keepdims=True) * (1.0 / (parts * width))
            inverse_rms = jnp.broadcast_to(lax.rsqrt(mean + norm_eps), (NORM_ROWS, HEAD))
            for part in range(parts):
                for block in range(width // HEAD):
                    first = part * width + block * HEAD
                    value = hid[part, rows, block * HEAD:(block + 1) * HEAD].astype(f32)
                    value = value * inverse_rms * gains[:, first:first + HEAD]
                    normed[placed, first:first + HEAD] = value.astype(bf16)
            return carry

        lax.fori_loop(0, CHUNK // NORM_ROWS, some_rows, 0)

    def project(group):
        for n, chunk in enumerate(group):
            normalise(chunk, n)
        ready = normed[0:len(group) * CHUNK, :]
        kv_all = jnp.dot(ready, wkv[...], preferred_element_type=f32)
        is_query = group[0] >= first_query
        if is_query:
            q_all = jnp.dot(ready, wq[...], preferred_element_type=f32)
        per_span = SPAN // CHUNK
        for n, chunk in enumerate(group):
            rows = pl.ds(chunk * CHUNK, CHUNK)
            here = slice(n * CHUNK, (n + 1) * CHUNK)
            angle = row_angles(chunk)
            cosine, sine = jnp.cos(angle), jnp.sin(angle)
            sine = jnp.where(lax.broadcasted_iota(jnp.int32, angle.shape, 1) < HALF, -sine, sine)
            new_key = rotate(kv_all[here, :HEAD], cosine, sine).astype(bf16)
            new_value = kv_all[here, HEAD:].astype(bf16)
            place = pl.ds(chunk % per_span * CHUNK, CHUNK)
            cached[own_slot, chunk // per_span, 0, place, :] = new_key
            cached[own_slot, chunk // per_span, 1, place, :] = new_value
            if is_query:
                for g in range(heads):
                    q_rows = pl.ds(g * SPAN + (chunk - first_query) * CHUNK, CHUNK)
                    q = q_all[here, g * HEAD:(g + 1) * HEAD]
                    queries[q_rows, :] = rotate(q, cosine, sine).astype(bf16)
            else:
                fresh_out[rows, :HEAD] = new_key
                fresh_out[rows, HEAD:] = new_value

    exponent = HEAD ** (-0.5) * LOG2E
    halves, _, query_block, _ = scores.shape

    def attend_group(slot, bias, causal):
        for n in range(halves):
            q = queries[n * query_block:(n + 1) * query_block, :]
            for i in range(stored):
                scores[n, i] = lax.dot_general(
                    q, cached[slot, i, 0], (((1,), (1,)), ((), ())), preferred_element_type=f32
                )
        for n in range(halves):
            for tile in range(query_block // TILE):
                here = slice(tile * TILE, (tile + 1) * TILE)
                rows = slice(n * query_block + tile * TILE, n * query_block + (tile + 1) * TILE)

                def part(i, side):
                    value = scores[n, i, here, side * HEAD:(side + 1) * HEAD]
                    if bias is not None:
                        return value + bias[i][:, side * HEAD:(side + 1) * HEAD]
                    if causal and i == stored - 1:
                        query_index = lax.broadcasted_iota(jnp.int32, (TILE, HEAD), 0) + tile * TILE % SPAN
                        key_index = lax.broadcasted_iota(jnp.int32, (TILE, HEAD), 1) + side * HEAD
                        return jnp.where(key_index <= query_index, value, MASKED)
                    return value

                before = top[rows, :]
                peak = before
                for i in range(stored):
                    peak = jnp.maximum(peak, jnp.maximum(part(i, 0), part(i, 1)))
                peak = jnp.broadcast_to(jnp.max(peak, axis=1, keepdims=True), (TILE, HEAD))
                top[rows, :] = peak
                fade = jnp.exp2((before - peak) * exponent)
                sums = total[rows, :] * fade
                for i in range(stored):
                    for side in range(2):
                        weight = jnp.exp2((part(i, side) - peak) * exponent)
                        sums = sums + weight
                        weights[n, i, here, side * HEAD:(side + 1) * HEAD] = weight.astype(bf16)
                total[rows, :] = sums
                mixed[rows, :] = mixed[rows, :] * fade
            rows = slice(n * query_block, (n + 1) * query_block)
            gained = jnp.dot(weights[n, 0], cached[slot, 0, 1], preferred_element_type=f32)
            for i in range(1, stored):
                gained = gained + jnp.dot(weights[n, i], cached[slot, i, 1], preferred_element_type=f32)
            mixed[rows, :] += gained

    def keep_cached(slot):
        return pltpu.make_async_copy(cached.at[slot], cached_out.at[slot], cached_sem.at[slot])

    def span_group(slot):
        bias = []
        for i in range(stored):
            position = slot * stored + i
            doc = table_rows - 1
            for j in range(MAXDOC):
                doc = doc + jnp.where(positions[j] == position, j - (table_rows - 1), 0)
            doc = jnp.clip(doc, 0, table_rows - 1)
            cosine, sine = doc_cos[pl.ds(doc, 1), :], doc_sin[pl.ds(doc, 1), :]
            bias.append(hidden_rows[pl.ds(doc, 1), :])
            for b in range(blocks):
                rows = slice(b * SB, (b + 1) * SB)
                first = i * 2 * blocks + b
                k = codes_all[slot, i, 0, rows, :].astype(f32) * scales_all[slot, first:first + 1, :]
                cached[slot, i, 0, rows, :] = rotate(k, cosine, sine).astype(bf16)
                first = first + blocks
                v = codes_all[slot, i, 1, rows, :].astype(f32) * scales_all[slot, first:first + 1, :]
                cached[slot, i, 1, rows, :] = v.astype(bf16)
        keep_cached(slot).start()
        attend_group(slot, bias, False)

    def span_step(k):
        @pl.when(z >= k)
        def _():
            for copy in up(False, z - k):
                copy.wait_recv()
            start_all(over(False, z - k))
            pl.when(z < last)(lambda: start_all(up(False, z - k)))

        @pl.when(z + k <= last)
        def _():
            for copy in down(False, z + k):
                copy.wait_recv()
            start_all(over(False, z + k))
            pl.when(z > 0)(lambda: start_all(down(False, z + k)))

    folded = jnp.where(z < 2, z, last - z)

    def near(k):
        owner = jnp.where(folded == 0, k, (1, 0, 2, 3)[k])
        return jnp.where(z < 2, owner, last - owner)

    def same_column(k):
        span_group(near(k) * 2 + x)

    def other_column(k):
        for copy in span_copies(False, near(k), 1 - x, x_send, x_recv, x_peer):
            copy.wait_recv()
        span_group(near(k) * 2 + 1 - x)

    def relay(i):
        hidden_arrival(0, order[i])
        hidden_copy(2, order[i]).start()

    scales_all[s] = scales_own[...]
    relay(0)
    span_step(1)
    relay(1)
    project(order[0:2])
    same_column(0)
    relay(2)
    span_step(2)
    other_column(0)
    same_column(1)
    relay(3)
    span_step(3)
    project(order[2:4])
    other_column(1)
    relay(4)
    same_column(2)
    same_column(3)
    relay(5)
    project(order[4:6])
    other_column(2)
    attend_group(own_slot, None, True)
    other_column(3)

    live = lax.broadcasted_iota(jnp.int32, (SPAN, HEAD), 0) < query_len[0]
    for g in range(heads):
        rows = pl.ds(g * SPAN, SPAN)
        result = mixed[rows, :] / jnp.sum(total[rows, :], axis=1, keepdims=True)
        attn_out[:, g * HEAD:(g + 1) * HEAD] = jnp.where(live, result, 0.0).astype(bf16)

    for slot in range(own_slot):
        keep_cached(slot).wait()
    for chunk in range(chunks):
        for kind in range(3):
            hidden_copy(kind, chunk).wait_send()
    for owner in range(4):
        for copy in over(False, owner):
            copy.wait_send()

        @pl.when(jnp.logical_and(z < last, owner <= z))
        def _():
            for copy in up(False, owner):
                copy.wait_send()

        @pl.when(jnp.logical_and(z > 0, owner >= z))
        def _():
            for copy in down(False, owner):
                copy.wait_send()


def stream(peers, tp, home, ids, count, query_len, hidden, codes, scales, w_q, w_kv, gain, recompute):
    rows, width = hidden.shape
    features = w_q.shape[0]
    heads = w_q.shape[1] // HEAD
    chunks = rows // CHUNK
    table_rows = 32
    doc_cos, doc_sin = doc_tables(table_rows)
    fresh = rows - SPAN
    dma = pltpu.SemaphoreType.DMA
    return pl.pallas_call(
        stream_kernel,
        out_shape=(
            jax.ShapeDtypeStruct((SPAN, heads * HEAD), bf16),
            jax.ShapeDtypeStruct((fresh, 2 * HEAD), bf16),
            jax.ShapeDtypeStruct((peers,) + codes.shape, bf16),
        ),
        in_specs=[SMEM] * 4 + [ANY, ANY, VMEM, ANY, ANY] + [VMEM] * 5,
        out_specs=(VMEM, VMEM, ANY),
        scratch_shapes=[
            pltpu.VMEM((tp, rows, width), bf16),
            pltpu.VMEM((features, w_q.shape[1]), bf16),
            pltpu.VMEM((2 * features, HEAD), bf16),
            pltpu.VMEM((features, 2 * HEAD), bf16),
            pltpu.VMEM((512, HEAD), f32),
            pltpu.VMEM((peers,) + codes.shape, bf16),
            pltpu.VMEM((SCALE_ROWS, HEAD), f32),
            pltpu.VMEM((peers, SCALE_ROWS, HEAD), f32),
            pltpu.VMEM((peers + 1,) + codes.shape, bf16),
            pltpu.VMEM((heads * SPAN, HEAD), bf16),
            pltpu.VMEM((heads // 2, codes.shape[0], 2 * SPAN, SPAN), f32),
            pltpu.VMEM((heads // 2, codes.shape[0], 2 * SPAN, SPAN), bf16),
            pltpu.VMEM((SPAN, features), bf16),
            pltpu.VMEM((1, features), f32),
            pltpu.VMEM((heads * SPAN, HEAD), f32),
            pltpu.VMEM((heads * SPAN, HEAD), f32),
            pltpu.VMEM((heads * SPAN, HEAD), f32),
            pltpu.VMEM((table_rows, SPAN), f32),
            dma((4,)),
            dma((peers,)),
            dma((3, chunks)),
            dma((3, chunks)),
            dma((4, 2)),
            dma((4, 2)),
            dma((4, 2)),
            dma((4, 2)),
            dma((4, 2)),
        ],
        compiler_params=pltpu.CompilerParams(
            collective_id=0, has_side_effects=True, vmem_limit_bytes=60 * 2**20
        ),
        name="stream_attend",
    )(home, ids, count, query_len, hidden, codes, scales, w_q, w_kv, gain, recompute,
      inverse_freq()[None, :], doc_cos, doc_sin)


def place_kernel(
    home, ids, count, recompute, attended, cached, fresh,
    out, context,
    fetched, placed, fetch_sem, write_sem, out_sem,
):
    docs = count[0]
    passed = pltpu.make_async_copy(attended, out, out_sem)
    passed.start()

    def fetch(j):
        return pltpu.make_async_copy(cached.at[home[ids[0, j]]], fetched.at[j], fetch_sem.at[j])

    def write(j, part):
        rows = pl.ds(pl.multiple_of(j * SPAN, SPAN), SPAN)
        return pltpu.make_async_copy(placed.at[j, part], context.at[part, rows], write_sem.at[j, part])

    lax.fori_loop(0, docs, lambda j, n: (fetch(j).start(), n)[1], 0)
    ones = jnp.ones((fresh.shape[0], HEAD), bf16)

    def fill(j, carry):
        @pl.when(j < docs)
        def _():
            rows = lax.broadcasted_iota(jnp.int32, (SPAN, CHUNK), 0) + j * SPAN
            match = jnp.concatenate(
                [
                    jnp.where(recompute[r:r + 1, :] == rows, 1.0, 0.0).astype(bf16)
                    for r in range(recompute.shape[0])
                ],
                axis=1,
            )
            hit = jnp.dot(match, ones, preferred_element_type=f32) > 0.5
            patch = jnp.dot(match, fresh[...], preferred_element_type=f32)
            fetch(j).wait()
            for part in range(2):
                new = patch[:, part * HEAD:(part + 1) * HEAD]
                placed[j, part] = jnp.where(hit, new, fetched[j, part].astype(f32)).astype(bf16)

        @pl.when(j >= docs)
        def _():
            placed[j] = jnp.zeros(placed.shape[1:], bf16)

        write(j, 0).start()
        write(j, 1).start()
        return carry

    lax.fori_loop(0, MAXDOC, fill, 0)

    def drain(j, carry):
        write(j, 0).wait()
        write(j, 1).wait()
        return carry

    lax.fori_loop(0, MAXDOC, drain, 0)
    passed.wait()


def place(home, ids, count, recompute, attended, cached, fresh):
    context_max = MAXDOC * SPAN
    return pl.pallas_call(
        place_kernel,
        out_shape=(
            jax.ShapeDtypeStruct(attended.shape, bf16),
            jax.ShapeDtypeStruct((2, context_max, HEAD), bf16),
        ),
        in_specs=[SMEM] * 3 + [VMEM, ANY, ANY, VMEM],
        out_specs=(ANY, ANY),
        scratch_shapes=[
            pltpu.VMEM((MAXDOC, 2, SPAN, HEAD), bf16),
            pltpu.VMEM((MAXDOC, 2, SPAN, HEAD), bf16),
            pltpu.SemaphoreType.DMA((MAXDOC,)),
            pltpu.SemaphoreType.DMA((MAXDOC, 2)),
            pltpu.SemaphoreType.DMA,
        ],
        compiler_params=pltpu.CompilerParams(vmem_limit_bytes=60 * 2**20),
        name="place_context",
    )(home, ids, count, recompute, attended, cached, fresh)


def plain_gather_and_project(hidden, codes, scales, w_q, w_kv, gain, angles):
    rows = hidden.shape[0]
    heads = w_q.shape[1] // HEAD
    all_codes = lax.all_gather(codes, "store", axis=0)
    all_scales = lax.all_gather(scales, "store", axis=0)
    features = lax.all_gather(hidden, "tp", axis=1, tiled=True).astype(f32)
    inverse_rms = lax.rsqrt(jnp.mean(features * features, axis=-1, keepdims=True) + norm_eps)
    normed = (features * inverse_rms * gain).astype(bf16)
    cosine, sine = jnp.cos(angles), jnp.sin(angles)
    sine = jnp.where(jnp.arange(HEAD)[None, :] < HALF, -sine, sine)
    kv = jnp.dot(normed, w_kv.reshape(-1, 2 * HEAD), preferred_element_type=f32)
    q = jnp.dot(normed[rows - SPAN:], w_q, preferred_element_type=f32)
    q = jnp.transpose(q.reshape(SPAN, heads, HEAD), (1, 0, 2))

    def turn(values, cosine, sine):
        return values * cosine + jnp.roll(values, HALF, axis=-1) * sine

    new_keys = turn(kv[:, :HEAD], cosine, sine)
    q = turn(q, cosine[rows - SPAN:], sine[rows - SPAN:]).astype(bf16)
    return q, new_keys, kv[:, HEAD:], all_codes, all_scales


def attend_kernel(
    stored, home, ids, count, recompute, query_len, codes, scales, doc_cos, doc_sin, q, new_k, new_v,
    out, context,
    fetched, scale_rows, key_rows, value_rows, keys, values, scores, top, total, mixed, fetch_sem, out_sem,
):
    docs = count[0]
    recompute_total = recompute.shape[0]
    context_max = MAXDOC * SPAN
    heads = q.shape[0]

    def fetch(j):
        position = home[ids[0, j]]
        return pltpu.make_async_copy(codes.at[position], fetched.at[j], fetch_sem.at[j])

    lax.fori_loop(0, docs, lambda j, n: (fetch(j).start(), n)[1], 0)
    scale_rows[...] = scales[...].astype(f32)

    def dequantise(j, carry):
        base = pl.multiple_of(j * SPAN, SPAN)

        @pl.when(j < docs)
        def _():
            fetch(j).wait()
            position = home[ids[0, j]]
            first = (position // stored) * SCALE_ROWS + (position % stored) * 4
            cosine, sine = doc_cos[pl.ds(j, 1), :], doc_sin[pl.ds(j, 1), :]
            for b in range(SPAN // SB):
                rows = pl.ds(base + b * SB, SB)
                k = fetched[j, 0, b * SB:(b + 1) * SB, :].astype(f32) * scale_rows[pl.ds(first + b, 1), :]
                key_rows[rows, :] = rotate(k, cosine, sine)
                v = fetched[j, 1, b * SB:(b + 1) * SB, :].astype(f32) * scale_rows[pl.ds(first + 2 + b, 1), :]
                value_rows[rows, :] = v

        @pl.when(j >= docs)
        def _():
            key_rows[pl.ds(base, SPAN), :] = jnp.zeros((SPAN, HEAD), f32)
            value_rows[pl.ds(base, SPAN), :] = jnp.zeros((SPAN, HEAD), f32)

        return carry

    lax.fori_loop(0, MAXDOC, dequantise, 0)

    def patch(i, carry):
        for u in range(8):
            source = i * 8 + u
            row = recompute[source]
            key_rows[pl.ds(row, 1), :] = new_k[pl.ds(source, 1), :]
            value_rows[pl.ds(row, 1), :] = new_v[pl.ds(source, 1), :]
        return carry

    lax.fori_loop(0, recompute_total // 8, patch, 0)

    def narrow(j, carry):
        rows = pl.ds(pl.multiple_of(j * SPAN, SPAN), SPAN)
        keys[rows, :] = key_rows[rows, :].astype(bf16)
        values[rows, :] = value_rows[rows, :].astype(bf16)
        return carry

    lax.fori_loop(0, MAXDOC, narrow, 0)
    keys[context_max:context_max + SPAN, :] = new_k[recompute_total:, :].astype(bf16)
    values[context_max:context_max + SPAN, :] = new_v[recompute_total:, :].astype(bf16)
    writes = [
        pltpu.make_async_copy(keys.at[0:context_max], context.at[0], out_sem.at[0]),
        pltpu.make_async_copy(values.at[0:context_max], context.at[1], out_sem.at[1]),
    ]
    for copy in writes:
        copy.start()

    def score(g, rows):
        return lax.dot_general(q[g], keys[rows, :], (((1,), (1,)), ((), ())), preferred_element_type=f32)

    own_rows = pl.ds(context_max, SPAN)
    query_index = lax.broadcasted_iota(jnp.int32, (SPAN, SPAN), 0)
    key_index = lax.broadcasted_iota(jnp.int32, (SPAN, SPAN), 1)
    for g in range(heads):
        own = jnp.where(key_index <= query_index, score(g, own_rows), -1e30)
        scores[MAXDOC, g] = own
        top[g] = jnp.maximum(own[:, :HEAD], own[:, HEAD:])

    def first_pass(j, carry):
        rows = pl.ds(pl.multiple_of(j * SPAN, SPAN), SPAN)
        for g in range(heads):
            block = score(g, rows)
            scores[j, g] = block
            top[g] = jnp.maximum(top[g], jnp.maximum(block[:, :HEAD], block[:, HEAD:]))
        return carry

    lax.fori_loop(0, docs, first_pass, 0)
    for g in range(heads):
        top[g] = jnp.broadcast_to(jnp.max(top[g], axis=1, keepdims=True), (SPAN, HEAD))
        total[g] = jnp.zeros((SPAN, HEAD), f32)
        mixed[g] = jnp.zeros((SPAN, HEAD), f32)

    def weigh(slot, rows):
        for g in range(heads):
            peak = top[g]
            low = jnp.exp((scores[slot, g, :, :HEAD] - peak) * HEAD ** (-0.5))
            high = jnp.exp((scores[slot, g, :, HEAD:] - peak) * HEAD ** (-0.5))
            total[g] += low + high
            weights = jnp.concatenate([low.astype(bf16), high.astype(bf16)], axis=1)
            mixed[g] += jnp.dot(weights, values[rows, :], preferred_element_type=f32)

    def second_pass(j, carry):
        weigh(j, pl.ds(pl.multiple_of(j * SPAN, SPAN), SPAN))
        return carry

    lax.fori_loop(0, docs, second_pass, 0)
    weigh(MAXDOC, own_rows)
    live = lax.broadcasted_iota(jnp.int32, (SPAN, HEAD), 0) < query_len[0]
    for g in range(heads):
        result = mixed[g] / jnp.sum(total[g], axis=1, keepdims=True)
        out[:, g * HEAD:(g + 1) * HEAD] = jnp.where(live, result, 0.0).astype(bf16)
    for copy in writes:
        copy.wait()


def attend(stored, home, ids, count, recompute, query_len, codes, scales, q, new_k, new_v):
    context_max = MAXDOC * SPAN
    heads = q.shape[0]
    freq = inverse_freq()
    angle = ((np.arange(24) * SPAN).astype(np.float32)[:, None] * freq[None, :]).astype(np.float64)
    sign = np.where(np.arange(HEAD) < HALF, -1.0, 1.0)
    doc_cos = np.cos(angle).astype(np.float32)
    doc_sin = (np.sin(angle) * sign).astype(np.float32)
    return pl.pallas_call(
        functools.partial(attend_kernel, stored),
        out_shape=(
            jax.ShapeDtypeStruct((SPAN, heads * HEAD), bf16),
            jax.ShapeDtypeStruct((2, context_max, HEAD), bf16),
        ),
        in_specs=[SMEM] * 5 + [ANY] + [VMEM] * 6,
        out_specs=(VMEM, ANY),
        scratch_shapes=[
            pltpu.VMEM((MAXDOC, 2, SPAN, HEAD), bf16),
            pltpu.VMEM(scales.shape, f32),
            pltpu.VMEM((context_max, HEAD), f32),
            pltpu.VMEM((context_max, HEAD), f32),
            pltpu.VMEM((context_max + SPAN, HEAD), bf16),
            pltpu.VMEM((context_max + SPAN, HEAD), bf16),
            pltpu.VMEM((MAXDOC + 1, heads, SPAN, SPAN), f32),
            pltpu.VMEM((heads, SPAN, HEAD), f32),
            pltpu.VMEM((heads, SPAN, HEAD), f32),
            pltpu.VMEM((heads, SPAN, HEAD), f32),
            pltpu.SemaphoreType.DMA((MAXDOC,)),
            pltpu.SemaphoreType.DMA((2,)),
        ],
        compiler_params=pltpu.CompilerParams(vmem_limit_bytes=48 * 2**20),
        name="patch_attend",
    )(home, ids, count, recompute, query_len, codes, scales, doc_cos, doc_sin, q, new_k, new_v)


def on_device(
    kv_store, kv_scale, span_home, doc_ids, doc_count, recompute_rows, query_len, hidden, norm_gain, w_q, w_kv,
):
    peers, tp = lax.axis_size("store"), lax.axis_size("tp")
    stored = kv_store.shape[0]
    gain = norm_gain.astype(f32).reshape(1, -1)
    pairs = w_kv.reshape(-1, HEAD)
    if (peers, tp) == (8, 4):
        attended, fresh, cached = stream(
            peers, tp, span_home, doc_ids, doc_count, query_len, hidden[0], kv_store,
            jnp.transpose(kv_scale, (2, 1, 3, 0)), w_q, pairs, norm_gain, recompute_rows[0],
        )
        cached = cached.reshape((peers * stored,) + kv_store.shape[1:])
        attention, context = place(
            span_home, doc_ids, doc_count, recompute_rows[0], attended, cached, fresh
        )
        return attention[None], context[None]
    scales = jnp.broadcast_to(kv_scale.reshape(stored * 4, 1), (stored * 4, HEAD))
    scales = jnp.pad(scales, ((0, SCALE_ROWS - stored * 4), (0, 0)))
    flat = recompute_rows.reshape(-1)
    row_pos = jnp.concatenate([flat, doc_count[0] * SPAN + jnp.arange(SPAN, dtype=jnp.int32)])
    angles = row_pos.astype(f32)[:, None] * inverse_freq()[None, :]
    gathered = plain_gather_and_project(hidden[0], kv_store, scales, w_q, pairs, gain, angles)
    q, new_k, new_v, codes, all_scales = gathered
    attention, context = attend(
        stored, span_home, doc_ids, doc_count, flat, query_len,
        codes.reshape((peers * stored,) + kv_store.shape[1:]), all_scales.reshape(-1, HEAD), q, new_k, new_v,
    )
    return attention[None], context[None]


def solution(mesh):
    placed = (
        P("store", None, None, "tp"),
        P("store", None, "tp", None),
        P(),
        P("store", None),
        P("store"),
        P("store", None, None),
        P("store"),
        P("store", None, "tp"),
        P(),
        P(None, "tp"),
        P(None, None, "tp"),
    )
    return jax.shard_map(
        on_device,
        mesh=mesh,
        in_specs=placed,
        out_specs=(P("store", None, "tp"), P("store", None, None, "tp")),
        check_vma=False,
    )
```

```python
import functools

import jax
import jax.numpy as jnp
import numpy as np
from jax import lax
from jax.experimental import pallas as pl
from jax.experimental.pallas import tpu as pltpu
from jax.sharding import PartitionSpec as P

SPAN = 256
SB = 128
MAXDOC = 20
HEAD = 128
HALF = HEAD // 2
CHUNK = 128
SCALE_ROWS = 16
rope_base = 500000.0
norm_eps = 1e-05
MASKED = -1e30
LOG2E = 1.4426950408889634
NORM_ROWS = 16
f32, bf16 = jnp.float32, jnp.bfloat16
MESH = pl.DeviceIdType.MESH
ANY = pl.BlockSpec(memory_space=pl.ANY)
VMEM = pl.BlockSpec(memory_space=pltpu.VMEM)
SMEM = pl.BlockSpec(memory_space=pltpu.SMEM)


def inverse_freq():
    half = np.power(rope_base, -np.arange(HALF) * (2.0 / HEAD)).astype(np.float32)
    return np.concatenate([half, half])


def rotate(values, cosine, signed_sine):
    return values * cosine + pltpu.roll(values, HALF, 1) * signed_sine


def doc_tables(rows):
    angle = ((np.arange(rows) * SPAN).astype(np.float32)[:, None] * inverse_freq()[None, :]).astype(np.float64)
    sign = np.where(np.arange(HEAD) < HALF, -1.0, 1.0)
    return np.cos(angle).astype(np.float32), (np.sin(angle) * sign).astype(np.float32)


def stream_kernel(
    home, ids, count, query_len, hidden, codes, scales, w_q, w_kv, gain, recompute, freq, doc_cos, doc_sin,
    attn_out, fresh_out, cached_out,
    hid, wq, wkv_raw, wkv, wide, codes_all, scales_own, scales_all, cached, queries, scores, normed, gains,
    top, total, mixed, hidden_rows,
    local_sem, cached_sem, hid_send, hid_recv, up_send, down_send, x_send, z_recv, x_recv,
):
    s = lax.axis_index("store")
    t = lax.axis_index("tp")
    z, x = s // 2, s % 2
    y, c = t // 2, t % 2
    last = 3
    across = (1 - y) * 2 + c
    sibling = y * 2 + (1 - c)
    diagonal = (1 - y) * 2 + (1 - c)
    x_peer = z * 2 + (1 - x)

    barrier = pltpu.get_barrier_semaphore()

    def greet(axis, index):
        pl.semaphore_signal(barrier, inc=1, device_id={axis: index}, device_id_type=MESH)

    greet("tp", across)
    greet("tp", sibling)
    greet("store", x_peer)
    pl.when(z > 0)(lambda: greet("store", s - 2))
    pl.when(z < last)(lambda: greet("store", s + 2))

    local = [
        pltpu.make_async_copy(w_kv, wkv_raw, local_sem.at[0]),
        pltpu.make_async_copy(w_q, wq, local_sem.at[1]),
        pltpu.make_async_copy(hidden, hid.at[t], local_sem.at[2]),
        pltpu.make_async_copy(codes, codes_all.at[s], local_sem.at[3]),
    ]

    def start_all(copies):
        for copy in copies:
            copy.start()

    start_all(local)
    stored, blocks = codes.shape[0], SPAN // SB
    scales_own[...] = jnp.zeros(scales_own.shape, f32)
    for i in range(stored):
        for part in range(2):
            pair = scales[0, part].astype(f32)
            for b in range(blocks):
                row = (i * 2 + part) * blocks + b
                scales_own[row:row + 1, :] = jnp.broadcast_to(pair[b:b + 1, i:i + 1], (1, HEAD))
    pl.semaphore_wait(barrier, 3 + jnp.where(z > 0, 1, 0) + jnp.where(z < last, 1, 0))

    def span_copies(own, owner_z, column, send, recv, target):
        slot = owner_z * 2 + column
        pairs = ((codes if own else codes_all.at[slot], codes_all.at[slot], 0),
                 (scales_own if own else scales_all.at[slot], scales_all.at[slot], 1))
        return [
            pltpu.make_async_remote_copy(
                src_ref=src, dst_ref=dst, send_sem=send.at[owner_z, i], recv_sem=recv.at[owner_z, i],
                device_id={"store": target}, device_id_type=MESH,
            )
            for src, dst, i in pairs
        ]

    def up(own, owner_z):
        return span_copies(own, owner_z, x, up_send, z_recv, s + 2)

    def down(own, owner_z):
        return span_copies(own, owner_z, x, down_send, z_recv, s - 2)

    def over(own, owner_z):
        return span_copies(own, owner_z, x, x_send, x_recv, x_peer)

    def hidden_copy(kind, chunk):
        rows = pl.ds(chunk * CHUNK, CHUNK)
        slot = across if kind == 2 else t
        return pltpu.make_async_remote_copy(
            src_ref=hid.at[slot, rows] if kind == 2 else hidden.at[rows],
            dst_ref=hid.at[slot, rows],
            send_sem=hid_send.at[kind, chunk], recv_sem=hid_recv.at[kind, chunk],
            device_id={"tp": across if kind == 0 else sibling}, device_id_type=MESH,
        )

    def hidden_arrival(kind, chunk):
        rows = pl.ds(chunk * CHUNK, CHUNK)
        slot = (across, sibling, diagonal)[kind]
        pltpu.make_async_remote_copy(
            src_ref=hidden.at[rows], dst_ref=hid.at[slot, rows],
            send_sem=hid_send.at[kind, chunk], recv_sem=hid_recv.at[kind, chunk],
            device_id={"tp": across if kind == 0 else sibling}, device_id_type=MESH,
        ).wait_recv()

    chunks = hidden.shape[0] // CHUNK
    query_chunks = SPAN // CHUNK
    first_query = chunks - query_chunks
    order = list(range(first_query, chunks)) + list(range(first_query))

    start_all(over(True, z))
    pl.when(z < last)(lambda: start_all(up(True, z)))
    pl.when(z > 0)(lambda: start_all(down(True, z)))
    for chunk in order:
        hidden_copy(0, chunk).start()
    for chunk in order:
        hidden_copy(1, chunk).start()

    gains[...] = gain[...].astype(f32).reshape(gains.shape)
    docs = count[0]
    positions = [home[ids[0, j]] for j in range(MAXDOC)]
    table_rows = hidden_rows.shape[0]
    hits = jnp.zeros((table_rows, SPAN), f32)
    for r in range(recompute.shape[0]):
        row = recompute[r:r + 1, :]
        doc_match = lax.broadcasted_iota(jnp.int32, (table_rows, CHUNK), 0) == (row >> 8)
        row_match = lax.broadcasted_iota(jnp.int32, (SPAN, CHUNK), 0) == (row & 255)
        hits = hits + lax.dot_general(
            jnp.where(doc_match, 1.0, 0.0).astype(bf16), jnp.where(row_match, 1.0, 0.0).astype(bf16),
            (((1,), (1,)), ((), ())), preferred_element_type=f32,
        )
    dead = lax.broadcasted_iota(jnp.int32, (table_rows, SPAN), 0) >= docs
    hidden_rows[...] = jnp.where(jnp.logical_or(dead, hits > 0.5), MASKED, 0.0)
    top[...] = jnp.full(top.shape, MASKED, f32)
    total[...] = jnp.zeros(total.shape, f32)
    mixed[...] = jnp.zeros(mixed.shape, f32)

    local[0].wait()
    block = wide.shape[0]

    def split_pairs(i, carry):
        wide[...] = wkv_raw[pl.ds(pl.multiple_of(i * block, block), block), :].astype(f32)
        rows = pl.ds(pl.multiple_of(i * (block // 2), block // 2), block // 2)
        wkv[rows, 0:HEAD] = wide[pl.ds(0, block // 2, stride=2), :].astype(bf16)
        wkv[rows, HEAD:2 * HEAD] = wide[pl.ds(1, block // 2, stride=2), :].astype(bf16)
        return carry

    lax.fori_loop(0, wkv_raw.shape[0] // block, split_pairs, 0)
    for copy in local[1:]:
        copy.wait()

    parts, _, width = hid.shape
    heads = wq.shape[1] // HEAD
    own_slot = cached.shape[0] - 1

    def row_angles(chunk):
        if chunk >= first_query:
            offset = docs * SPAN + (chunk - first_query) * CHUNK
            place = lax.broadcasted_iota(jnp.int32, (CHUNK, HEAD), 0) + offset
            return place.astype(f32) * freq[...]
        row = jnp.broadcast_to(recompute[chunk:chunk + 1, :].astype(f32), (CHUNK, CHUNK))
        down_rows = lax.broadcasted_iota(jnp.int32, (CHUNK, CHUNK), 0)
        diagonal_entry = down_rows == lax.broadcasted_iota(jnp.int32, (CHUNK, CHUNK), 1)
        return jnp.sum(jnp.where(diagonal_entry, row, 0.0), axis=1, keepdims=True) * freq[...]

    def normalise(chunk, place):
        hidden_arrival(1, chunk)
        hidden_arrival(2, chunk)

        def some_rows(i, carry):
            rows = pl.ds(pl.multiple_of(chunk * CHUNK + i * NORM_ROWS, NORM_ROWS), NORM_ROWS)
            placed = pl.ds(pl.multiple_of(place * CHUNK + i * NORM_ROWS, NORM_ROWS), NORM_ROWS)
            squares = jnp.zeros((NORM_ROWS, HEAD), f32)
            for part in range(parts):
                for block in range(width // HEAD):
                    value = hid[part, rows, block * HEAD:(block + 1) * HEAD].astype(f32)
                    squares = squares + value * value
            mean = jnp.sum(squares, axis=1, keepdims=True) * (1.0 / (parts * width))
            inverse_rms = jnp.broadcast_to(lax.rsqrt(mean + norm_eps), (NORM_ROWS, HEAD))
            for part in range(parts):
                for block in range(width // HEAD):
                    first = part * width + block * HEAD
                    value = hid[part, rows, block * HEAD:(block + 1) * HEAD].astype(f32)
                    value = value * inverse_rms * gains[:, first:first + HEAD]
                    normed[placed, first:first + HEAD] = value.astype(bf16)
            return carry

        lax.fori_loop(0, CHUNK // NORM_ROWS, some_rows, 0)

    def project(group):
        for n, chunk in enumerate(group):
            normalise(chunk, n)
        ready = normed[0:len(group) * CHUNK, :]
        kv_all = jnp.dot(ready, wkv[...], preferred_element_type=f32)
        is_query = group[0] >= first_query
        if is_query:
            q_all = jnp.dot(ready, wq[...], preferred_element_type=f32)
        per_span = SPAN // CHUNK
        for n, chunk in enumerate(group):
            rows = pl.ds(chunk * CHUNK, CHUNK)
            here = slice(n * CHUNK, (n + 1) * CHUNK)
            angle = row_angles(chunk)
            cosine, sine = jnp.cos(angle), jnp.sin(angle)
            sine = jnp.where(lax.broadcasted_iota(jnp.int32, angle.shape, 1) < HALF, -sine, sine)
            new_key = rotate(kv_all[here, :HEAD], cosine, sine).astype(bf16)
            new_value = kv_all[here, HEAD:].astype(bf16)
            place = pl.ds(chunk % per_span * CHUNK, CHUNK)
            cached[own_slot, chunk // per_span, 0, place, :] = new_key
            cached[own_slot, chunk // per_span, 1, place, :] = new_value
            if is_query:
                for g in range(heads):
                    q_rows = pl.ds(g * SPAN + (chunk - first_query) * CHUNK, CHUNK)
                    q = q_all[here, g * HEAD:(g + 1) * HEAD]
                    queries[q_rows, :] = rotate(q, cosine, sine).astype(bf16)
            else:
                fresh_out[rows, :HEAD] = new_key
                fresh_out[rows, HEAD:] = new_value

    exponent = HEAD ** (-0.5) * LOG2E
    query_block = scores.shape[1]

    def attend_group(slot, bias, causal):
        def some_queries(n, carry):
            rows = pl.ds(pl.multiple_of(n * query_block, query_block), query_block)
            q = queries[rows, :]
            before = top[rows, :]
            peak = before
            for i in range(stored):
                part = lax.dot_general(
                    q, cached[slot, i, 0], (((1,), (1,)), ((), ())), preferred_element_type=f32
                )
                if bias is not None:
                    part = part + bias[i]
                elif causal and i == stored - 1:
                    query_index = lax.broadcasted_iota(jnp.int32, (query_block, SPAN), 0) & (SPAN - 1)
                    key_index = lax.broadcasted_iota(jnp.int32, (query_block, SPAN), 1)
                    part = jnp.where(key_index <= query_index, part, MASKED)
                scores[i] = part
                peak = jnp.maximum(peak, jnp.maximum(part[:, :HEAD], part[:, HEAD:]))
            peak = jnp.broadcast_to(jnp.max(peak, axis=1, keepdims=True), (query_block, HEAD))
            top[rows, :] = peak
            fade = jnp.exp2((before - peak) * exponent)
            sums = total[rows, :] * fade
            gained = jnp.zeros((query_block, HEAD), f32)
            for i in range(stored):
                low = jnp.exp2((scores[i, :, :HEAD] - peak) * exponent)
                high = jnp.exp2((scores[i, :, HEAD:] - peak) * exponent)
                sums = sums + (low + high)
                weights = jnp.concatenate([low.astype(bf16), high.astype(bf16)], axis=1)
                gained = gained + jnp.dot(weights, cached[slot, i, 1], preferred_element_type=f32)
            total[rows, :] = sums
            mixed[rows, :] = mixed[rows, :] * fade + gained
            return carry

        lax.fori_loop(0, queries.shape[0] // query_block, some_queries, 0)

    def keep_cached(slot):
        return pltpu.make_async_copy(cached.at[slot], cached_out.at[slot], cached_sem.at[slot])

    def span_group(slot):
        bias = []
        for i in range(stored):
            position = slot * stored + i
            doc = table_rows - 1
            for j in range(MAXDOC):
                doc = doc + jnp.where(positions[j] == position, j - (table_rows - 1), 0)
            doc = jnp.clip(doc, 0, table_rows - 1)
            cosine, sine = doc_cos[pl.ds(doc, 1), :], doc_sin[pl.ds(doc, 1), :]
            bias.append(hidden_rows[pl.ds(doc, 1), :])
            for b in range(blocks):
                rows = slice(b * SB, (b + 1) * SB)
                first = i * 2 * blocks + b
                k = codes_all[slot, i, 0, rows, :].astype(f32) * scales_all[slot, first:first + 1, :]
                cached[slot, i, 0, rows, :] = rotate(k, cosine, sine).astype(bf16)
                first = first + blocks
                v = codes_all[slot, i, 1, rows, :].astype(f32) * scales_all[slot, first:first + 1, :]
                cached[slot, i, 1, rows, :] = v.astype(bf16)
        keep_cached(slot).start()
        attend_group(slot, bias, False)

    def span_step(k):
        @pl.when(z >= k)
        def _():
            for copy in up(False, z - k):
                copy.wait_recv()
            start_all(over(False, z - k))
            pl.when(z < last)(lambda: start_all(up(False, z - k)))

        @pl.when(z + k <= last)
        def _():
            for copy in down(False, z + k):
                copy.wait_recv()
            start_all(over(False, z + k))
            pl.when(z > 0)(lambda: start_all(down(False, z + k)))

    folded = jnp.where(z < 2, z, last - z)

    def near(k):
        owner = jnp.where(folded == 0, k, (1, 0, 2, 3)[k])
        return jnp.where(z < 2, owner, last - owner)

    def same_column(k):
        span_group(near(k) * 2 + x)

    def other_column(k):
        for copy in span_copies(False, near(k), 1 - x, x_send, x_recv, x_peer):
            copy.wait_recv()
        span_group(near(k) * 2 + 1 - x)

    def relay(i):
        hidden_arrival(0, order[i])
        hidden_copy(2, order[i]).start()

    scales_all[s] = scales_own[...]
    relay(0)
    span_step(1)
    relay(1)
    project(order[0:2])
    same_column(0)
    relay(2)
    span_step(2)
    other_column(0)
    same_column(1)
    relay(3)
    span_step(3)
    project(order[2:4])
    other_column(1)
    relay(4)
    same_column(2)
    same_column(3)
    relay(5)
    project(order[4:6])
    other_column(2)
    attend_group(own_slot, None, True)
    other_column(3)

    live = lax.broadcasted_iota(jnp.int32, (SPAN, HEAD), 0) < query_len[0]
    for g in range(heads):
        rows = pl.ds(g * SPAN, SPAN)
        result = mixed[rows, :] / jnp.sum(total[rows, :], axis=1, keepdims=True)
        attn_out[:, g * HEAD:(g + 1) * HEAD] = jnp.where(live, result, 0.0).astype(bf16)

    for slot in range(own_slot):
        keep_cached(slot).wait()
    for chunk in range(chunks):
        for kind in range(3):
            hidden_copy(kind, chunk).wait_send()
    for owner in range(4):
        for copy in over(False, owner):
            copy.wait_send()

        @pl.when(jnp.logical_and(z < last, owner <= z))
        def _():
            for copy in up(False, owner):
                copy.wait_send()

        @pl.when(jnp.logical_and(z > 0, owner >= z))
        def _():
            for copy in down(False, owner):
                copy.wait_send()


def stream(peers, tp, home, ids, count, query_len, hidden, codes, scales, w_q, w_kv, gain, recompute):
    rows, width = hidden.shape
    features = w_q.shape[0]
    heads = w_q.shape[1] // HEAD
    chunks = rows // CHUNK
    table_rows = 32
    doc_cos, doc_sin = doc_tables(table_rows)
    fresh = rows - SPAN
    dma = pltpu.SemaphoreType.DMA
    return pl.pallas_call(
        stream_kernel,
        out_shape=(
            jax.ShapeDtypeStruct((SPAN, heads * HEAD), bf16),
            jax.ShapeDtypeStruct((fresh, 2 * HEAD), bf16),
            jax.ShapeDtypeStruct((peers,) + codes.shape, bf16),
        ),
        in_specs=[SMEM] * 4 + [ANY, ANY, VMEM, ANY, ANY] + [VMEM] * 5,
        out_specs=(VMEM, VMEM, ANY),
        scratch_shapes=[
            pltpu.VMEM((tp, rows, width), bf16),
            pltpu.VMEM((features, w_q.shape[1]), bf16),
            pltpu.VMEM((2 * features, HEAD), bf16),
            pltpu.VMEM((features, 2 * HEAD), bf16),
            pltpu.VMEM((512, HEAD), f32),
            pltpu.VMEM((peers,) + codes.shape, bf16),
            pltpu.VMEM((SCALE_ROWS, HEAD), f32),
            pltpu.VMEM((peers, SCALE_ROWS, HEAD), f32),
            pltpu.VMEM((peers + 1,) + codes.shape, bf16),
            pltpu.VMEM((heads * SPAN, HEAD), bf16),
            pltpu.VMEM((codes.shape[0], 2 * SPAN, SPAN), f32),
            pltpu.VMEM((SPAN, features), bf16),
            pltpu.VMEM((1, features), f32),
            pltpu.VMEM((heads * SPAN, HEAD), f32),
            pltpu.VMEM((heads * SPAN, HEAD), f32),
            pltpu.VMEM((heads * SPAN, HEAD), f32),
            pltpu.VMEM((table_rows, SPAN), f32),
            dma((4,)),
            dma((peers,)),
            dma((3, chunks)),
            dma((3, chunks)),
            dma((4, 2)),
            dma((4, 2)),
            dma((4, 2)),
            dma((4, 2)),
            dma((4, 2)),
        ],
        compiler_params=pltpu.CompilerParams(
            collective_id=0, has_side_effects=True, vmem_limit_bytes=60 * 2**20
        ),
        name="stream_attend",
    )(home, ids, count, query_len, hidden, codes, scales, w_q, w_kv, gain, recompute,
      inverse_freq()[None, :], doc_cos, doc_sin)


def place_kernel(
    home, ids, count, recompute, attended, cached, fresh,
    out, context,
    fetched, placed, fetch_sem, write_sem,
):
    docs = count[0]

    def fetch(j):
        return pltpu.make_async_copy(cached.at[home[ids[0, j]]], fetched.at[j], fetch_sem.at[j])

    def write(j, part):
        rows = pl.ds(pl.multiple_of(j * SPAN, SPAN), SPAN)
        return pltpu.make_async_copy(placed.at[j, part], context.at[part, rows], write_sem.at[j, part])

    lax.fori_loop(0, docs, lambda j, n: (fetch(j).start(), n)[1], 0)
    out[...] = attended[...]
    ones = jnp.ones((fresh.shape[0], HEAD), bf16)

    def fill(j, carry):
        @pl.when(j < docs)
        def _():
            rows = lax.broadcasted_iota(jnp.int32, (SPAN, CHUNK), 0) + j * SPAN
            match = jnp.concatenate(
                [
                    jnp.where(recompute[r:r + 1, :] == rows, 1.0, 0.0).astype(bf16)
                    for r in range(recompute.shape[0])
                ],
                axis=1,
            )
            hit = jnp.dot(match, ones, preferred_element_type=f32) > 0.5
            patch = jnp.dot(match, fresh[...], preferred_element_type=f32)
            fetch(j).wait()
            for part in range(2):
                new = patch[:, part * HEAD:(part + 1) * HEAD]
                placed[j, part] = jnp.where(hit, new, fetched[j, part].astype(f32)).astype(bf16)

        @pl.when(j >= docs)
        def _():
            placed[j] = jnp.zeros(placed.shape[1:], bf16)

        write(j, 0).start()
        write(j, 1).start()
        return carry

    lax.fori_loop(0, MAXDOC, fill, 0)

    def drain(j, carry):
        write(j, 0).wait()
        write(j, 1).wait()
        return carry

    lax.fori_loop(0, MAXDOC, drain, 0)


def place(home, ids, count, recompute, attended, cached, fresh):
    context_max = MAXDOC * SPAN
    return pl.pallas_call(
        place_kernel,
        out_shape=(
            jax.ShapeDtypeStruct(attended.shape, bf16),
            jax.ShapeDtypeStruct((2, context_max, HEAD), bf16),
        ),
        in_specs=[SMEM] * 3 + [VMEM, VMEM, ANY, VMEM],
        out_specs=(VMEM, ANY),
        scratch_shapes=[
            pltpu.VMEM((MAXDOC, 2, SPAN, HEAD), bf16),
            pltpu.VMEM((MAXDOC, 2, SPAN, HEAD), bf16),
            pltpu.SemaphoreType.DMA((MAXDOC,)),
            pltpu.SemaphoreType.DMA((MAXDOC, 2)),
        ],
        compiler_params=pltpu.CompilerParams(vmem_limit_bytes=60 * 2**20),
        name="place_context",
    )(home, ids, count, recompute, attended, cached, fresh)


def plain_gather_and_project(hidden, codes, scales, w_q, w_kv, gain, angles):
    rows = hidden.shape[0]
    heads = w_q.shape[1] // HEAD
    all_codes = lax.all_gather(codes, "store", axis=0)
    all_scales = lax.all_gather(scales, "store", axis=0)
    features = lax.all_gather(hidden, "tp", axis=1, tiled=True).astype(f32)
    inverse_rms = lax.rsqrt(jnp.mean(features * features, axis=-1, keepdims=True) + norm_eps)
    normed = (features * inverse_rms * gain).astype(bf16)
    cosine, sine = jnp.cos(angles), jnp.sin(angles)
    sine = jnp.where(jnp.arange(HEAD)[None, :] < HALF, -sine, sine)
    kv = jnp.dot(normed, w_kv.reshape(-1, 2 * HEAD), preferred_element_type=f32)
    q = jnp.dot(normed[rows - SPAN:], w_q, preferred_element_type=f32)
    q = jnp.transpose(q.reshape(SPAN, heads, HEAD), (1, 0, 2))

    def turn(values, cosine, sine):
        return values * cosine + jnp.roll(values, HALF, axis=-1) * sine

    new_keys = turn(kv[:, :HEAD], cosine, sine)
    q = turn(q, cosine[rows - SPAN:], sine[rows - SPAN:]).astype(bf16)
    return q, new_keys, kv[:, HEAD:], all_codes, all_scales


def attend_kernel(
    stored, home, ids, count, recompute, query_len, codes, scales, doc_cos, doc_sin, q, new_k, new_v,
    out, context,
    fetched, scale_rows, key_rows, value_rows, keys, values, scores, top, total, mixed, fetch_sem, out_sem,
):
    docs = count[0]
    recompute_total = recompute.shape[0]
    context_max = MAXDOC * SPAN
    heads = q.shape[0]

    def fetch(j):
        position = home[ids[0, j]]
        return pltpu.make_async_copy(codes.at[position], fetched.at[j], fetch_sem.at[j])

    lax.fori_loop(0, docs, lambda j, n: (fetch(j).start(), n)[1], 0)
    scale_rows[...] = scales[...].astype(f32)

    def dequantise(j, carry):
        base = pl.multiple_of(j * SPAN, SPAN)

        @pl.when(j < docs)
        def _():
            fetch(j).wait()
            position = home[ids[0, j]]
            first = (position // stored) * SCALE_ROWS + (position % stored) * 4
            cosine, sine = doc_cos[pl.ds(j, 1), :], doc_sin[pl.ds(j, 1), :]
            for b in range(SPAN // SB):
                rows = pl.ds(base + b * SB, SB)
                k = fetched[j, 0, b * SB:(b + 1) * SB, :].astype(f32) * scale_rows[pl.ds(first + b, 1), :]
                key_rows[rows, :] = rotate(k, cosine, sine)
                v = fetched[j, 1, b * SB:(b + 1) * SB, :].astype(f32) * scale_rows[pl.ds(first + 2 + b, 1), :]
                value_rows[rows, :] = v

        @pl.when(j >= docs)
        def _():
            key_rows[pl.ds(base, SPAN), :] = jnp.zeros((SPAN, HEAD), f32)
            value_rows[pl.ds(base, SPAN), :] = jnp.zeros((SPAN, HEAD), f32)

        return carry

    lax.fori_loop(0, MAXDOC, dequantise, 0)

    def patch(i, carry):
        for u in range(8):
            source = i * 8 + u
            row = recompute[source]
            key_rows[pl.ds(row, 1), :] = new_k[pl.ds(source, 1), :]
            value_rows[pl.ds(row, 1), :] = new_v[pl.ds(source, 1), :]
        return carry

    lax.fori_loop(0, recompute_total // 8, patch, 0)

    def narrow(j, carry):
        rows = pl.ds(pl.multiple_of(j * SPAN, SPAN), SPAN)
        keys[rows, :] = key_rows[rows, :].astype(bf16)
        values[rows, :] = value_rows[rows, :].astype(bf16)
        return carry

    lax.fori_loop(0, MAXDOC, narrow, 0)
    keys[context_max:context_max + SPAN, :] = new_k[recompute_total:, :].astype(bf16)
    values[context_max:context_max + SPAN, :] = new_v[recompute_total:, :].astype(bf16)
    writes = [
        pltpu.make_async_copy(keys.at[0:context_max], context.at[0], out_sem.at[0]),
        pltpu.make_async_copy(values.at[0:context_max], context.at[1], out_sem.at[1]),
    ]
    for copy in writes:
        copy.start()

    def score(g, rows):
        return lax.dot_general(q[g], keys[rows, :], (((1,), (1,)), ((), ())), preferred_element_type=f32)

    own_rows = pl.ds(context_max, SPAN)
    query_index = lax.broadcasted_iota(jnp.int32, (SPAN, SPAN), 0)
    key_index = lax.broadcasted_iota(jnp.int32, (SPAN, SPAN), 1)
    for g in range(heads):
        own = jnp.where(key_index <= query_index, score(g, own_rows), -1e30)
        scores[MAXDOC, g] = own
        top[g] = jnp.maximum(own[:, :HEAD], own[:, HEAD:])

    def first_pass(j, carry):
        rows = pl.ds(pl.multiple_of(j * SPAN, SPAN), SPAN)
        for g in range(heads):
            block = score(g, rows)
            scores[j, g] = block
            top[g] = jnp.maximum(top[g], jnp.maximum(block[:, :HEAD], block[:, HEAD:]))
        return carry

    lax.fori_loop(0, docs, first_pass, 0)
    for g in range(heads):
        top[g] = jnp.broadcast_to(jnp.max(top[g], axis=1, keepdims=True), (SPAN, HEAD))
        total[g] = jnp.zeros((SPAN, HEAD), f32)
        mixed[g] = jnp.zeros((SPAN, HEAD), f32)

    def weigh(slot, rows):
        for g in range(heads):
            peak = top[g]
            low = jnp.exp((scores[slot, g, :, :HEAD] - peak) * HEAD ** (-0.5))
            high = jnp.exp((scores[slot, g, :, HEAD:] - peak) * HEAD ** (-0.5))
            total[g] += low + high
            weights = jnp.concatenate([low.astype(bf16), high.astype(bf16)], axis=1)
            mixed[g] += jnp.dot(weights, values[rows, :], preferred_element_type=f32)

    def second_pass(j, carry):
        weigh(j, pl.ds(pl.multiple_of(j * SPAN, SPAN), SPAN))
        return carry

    lax.fori_loop(0, docs, second_pass, 0)
    weigh(MAXDOC, own_rows)
    live = lax.broadcasted_iota(jnp.int32, (SPAN, HEAD), 0) < query_len[0]
    for g in range(heads):
        result = mixed[g] / jnp.sum(total[g], axis=1, keepdims=True)
        out[:, g * HEAD:(g + 1) * HEAD] = jnp.where(live, result, 0.0).astype(bf16)
    for copy in writes:
        copy.wait()


def attend(stored, home, ids, count, recompute, query_len, codes, scales, q, new_k, new_v):
    context_max = MAXDOC * SPAN
    heads = q.shape[0]
    freq = inverse_freq()
    angle = ((np.arange(24) * SPAN).astype(np.float32)[:, None] * freq[None, :]).astype(np.float64)
    sign = np.where(np.arange(HEAD) < HALF, -1.0, 1.0)
    doc_cos = np.cos(angle).astype(np.float32)
    doc_sin = (np.sin(angle) * sign).astype(np.float32)
    return pl.pallas_call(
        functools.partial(attend_kernel, stored),
        out_shape=(
            jax.ShapeDtypeStruct((SPAN, heads * HEAD), bf16),
            jax.ShapeDtypeStruct((2, context_max, HEAD), bf16),
        ),
        in_specs=[SMEM] * 5 + [ANY] + [VMEM] * 6,
        out_specs=(VMEM, ANY),
        scratch_shapes=[
            pltpu.VMEM((MAXDOC, 2, SPAN, HEAD), bf16),
            pltpu.VMEM(scales.shape, f32),
            pltpu.VMEM((context_max, HEAD), f32),
            pltpu.VMEM((context_max, HEAD), f32),
            pltpu.VMEM((context_max + SPAN, HEAD), bf16),
            pltpu.VMEM((context_max + SPAN, HEAD), bf16),
            pltpu.VMEM((MAXDOC + 1, heads, SPAN, SPAN), f32),
            pltpu.VMEM((heads, SPAN, HEAD), f32),
            pltpu.VMEM((heads, SPAN, HEAD), f32),
            pltpu.VMEM((heads, SPAN, HEAD), f32),
            pltpu.SemaphoreType.DMA((MAXDOC,)),
            pltpu.SemaphoreType.DMA((2,)),
        ],
        compiler_params=pltpu.CompilerParams(vmem_limit_bytes=48 * 2**20),
        name="patch_attend",
    )(home, ids, count, recompute, query_len, codes, scales, doc_cos, doc_sin, q, new_k, new_v)


def on_device(
    kv_store, kv_scale, span_home, doc_ids, doc_count, recompute_rows, query_len, hidden, norm_gain, w_q, w_kv,
):
    peers, tp = lax.axis_size("store"), lax.axis_size("tp")
    stored = kv_store.shape[0]
    gain = norm_gain.astype(f32).reshape(1, -1)
    pairs = w_kv.reshape(-1, HEAD)
    if (peers, tp) == (8, 4):
        attended, fresh, cached = stream(
            peers, tp, span_home, doc_ids, doc_count, query_len, hidden[0], kv_store,
            jnp.transpose(kv_scale, (2, 1, 3, 0)), w_q, pairs, norm_gain, recompute_rows[0],
        )
        cached = cached.reshape((peers * stored,) + kv_store.shape[1:])
        attention, context = place(
            span_home, doc_ids, doc_count, recompute_rows[0], attended, cached, fresh
        )
        return attention[None], context[None]
    scales = jnp.broadcast_to(kv_scale.reshape(stored * 4, 1), (stored * 4, HEAD))
    scales = jnp.pad(scales, ((0, SCALE_ROWS - stored * 4), (0, 0)))
    flat = recompute_rows.reshape(-1)
    row_pos = jnp.concatenate([flat, doc_count[0] * SPAN + jnp.arange(SPAN, dtype=jnp.int32)])
    angles = row_pos.astype(f32)[:, None] * inverse_freq()[None, :]
    gathered = plain_gather_and_project(hidden[0], kv_store, scales, w_q, pairs, gain, angles)
    q, new_k, new_v, codes, all_scales = gathered
    attention, context = attend(
        stored, span_home, doc_ids, doc_count, flat, query_len,
        codes.reshape((peers * stored,) + kv_store.shape[1:]), all_scales.reshape(-1, HEAD), q, new_k, new_v,
    )
    return attention[None], context[None]


def solution(mesh):
    placed = (
        P("store", None, None, "tp"),
        P("store", None, "tp", None),
        P(),
        P("store", None),
        P("store"),
        P("store", None, None),
        P("store"),
        P("store", None, "tp"),
        P(),
        P(None, "tp"),
        P(None, None, "tp"),
    )
    return jax.shard_map(
        on_device,
        mesh=mesh,
        in_specs=placed,
        out_specs=(P("store", None, "tp"), P("store", None, None, "tp")),
        check_vma=False,
    )
```

```python
import functools

import jax
import jax.numpy as jnp
import numpy as np
from jax import lax
from jax.experimental import pallas as pl
from jax.experimental.pallas import tpu as pltpu
from jax.sharding import PartitionSpec as P

SPAN = 256
SB = 128
MAXDOC = 20
HEAD = 128
HALF = HEAD // 2
CHUNK = 128
SCALE_ROWS = 16
rope_base = 500000.0
norm_eps = 1e-05
MASKED = -1e30
LOG2E = 1.4426950408889634
NORM_ROWS = 16
f32, bf16 = jnp.float32, jnp.bfloat16
MESH = pl.DeviceIdType.MESH
ANY = pl.BlockSpec(memory_space=pl.ANY)
VMEM = pl.BlockSpec(memory_space=pltpu.VMEM)
SMEM = pl.BlockSpec(memory_space=pltpu.SMEM)


def inverse_freq():
    half = np.power(rope_base, -np.arange(HALF) * (2.0 / HEAD)).astype(np.float32)
    return np.concatenate([half, half])


def rotate(values, cosine, signed_sine):
    return values * cosine + pltpu.roll(values, HALF, 1) * signed_sine


def doc_tables(rows):
    angle = ((np.arange(rows) * SPAN).astype(np.float32)[:, None] * inverse_freq()[None, :]).astype(np.float64)
    sign = np.where(np.arange(HEAD) < HALF, -1.0, 1.0)
    return np.cos(angle).astype(np.float32), (np.sin(angle) * sign).astype(np.float32)


def stream_kernel(
    home, ids, count, query_len, hidden, codes, scales, w_q, w_kv, gain, recompute, freq, doc_cos, doc_sin,
    attn_out, fresh_out, cached_out,
    hid, wq, wkv_raw, wkv, wide, codes_all, scales_own, scales_all, cached, queries, scores, normed, gains,
    top, total, mixed, hidden_rows,
    local_sem, cached_sem, hid_send, hid_recv, up_send, down_send, x_send, z_recv, x_recv,
):
    s = lax.axis_index("store")
    t = lax.axis_index("tp")
    z, x = s // 2, s % 2
    y, c = t // 2, t % 2
    last = 3
    across = (1 - y) * 2 + c
    sibling = y * 2 + (1 - c)
    diagonal = (1 - y) * 2 + (1 - c)
    x_peer = z * 2 + (1 - x)

    barrier = pltpu.get_barrier_semaphore()

    def greet(axis, index):
        pl.semaphore_signal(barrier, inc=1, device_id={axis: index}, device_id_type=MESH)

    greet("tp", across)
    greet("tp", sibling)
    greet("store", x_peer)
    pl.when(z > 0)(lambda: greet("store", s - 2))
    pl.when(z < last)(lambda: greet("store", s + 2))

    local = [
        pltpu.make_async_copy(w_kv, wkv_raw, local_sem.at[0]),
        pltpu.make_async_copy(w_q, wq, local_sem.at[1]),
        pltpu.make_async_copy(hidden, hid.at[t], local_sem.at[2]),
        pltpu.make_async_copy(codes, codes_all.at[s], local_sem.at[3]),
    ]

    def start_all(copies):
        for copy in copies:
            copy.start()

    start_all(local)
    stored, blocks = codes.shape[0], SPAN // SB
    scales_own[...] = jnp.zeros(scales_own.shape, f32)
    for i in range(stored):
        for part in range(2):
            pair = scales[0, part].astype(f32)
            for b in range(blocks):
                row = (i * 2 + part) * blocks + b
                scales_own[row:row + 1, :] = jnp.broadcast_to(pair[b:b + 1, i:i + 1], (1, HEAD))
    pl.semaphore_wait(barrier, 3 + jnp.where(z > 0, 1, 0) + jnp.where(z < last, 1, 0))

    def span_copies(own, owner_z, column, send, recv, target):
        slot = owner_z * 2 + column
        pairs = ((codes if own else codes_all.at[slot], codes_all.at[slot], 0),
                 (scales_own if own else scales_all.at[slot], scales_all.at[slot], 1))
        return [
            pltpu.make_async_remote_copy(
                src_ref=src, dst_ref=dst, send_sem=send.at[owner_z, i], recv_sem=recv.at[owner_z, i],
                device_id={"store": target}, device_id_type=MESH,
            )
            for src, dst, i in pairs
        ]

    def up(own, owner_z):
        return span_copies(own, owner_z, x, up_send, z_recv, s + 2)

    def down(own, owner_z):
        return span_copies(own, owner_z, x, down_send, z_recv, s - 2)

    def over(own, owner_z):
        return span_copies(own, owner_z, x, x_send, x_recv, x_peer)

    def hidden_copy(kind, chunk):
        rows = pl.ds(chunk * CHUNK, CHUNK)
        slot = across if kind == 2 else t
        return pltpu.make_async_remote_copy(
            src_ref=hid.at[slot, rows] if kind == 2 else hidden.at[rows],
            dst_ref=hid.at[slot, rows],
            send_sem=hid_send.at[kind, chunk], recv_sem=hid_recv.at[kind, chunk],
            device_id={"tp": across if kind == 0 else sibling}, device_id_type=MESH,
        )

    def hidden_arrival(kind, chunk):
        rows = pl.ds(chunk * CHUNK, CHUNK)
        slot = (across, sibling, diagonal)[kind]
        pltpu.make_async_remote_copy(
            src_ref=hidden.at[rows], dst_ref=hid.at[slot, rows],
            send_sem=hid_send.at[kind, chunk], recv_sem=hid_recv.at[kind, chunk],
            device_id={"tp": across if kind == 0 else sibling}, device_id_type=MESH,
        ).wait_recv()

    chunks = hidden.shape[0] // CHUNK
    query_chunks = SPAN // CHUNK
    first_query = chunks - query_chunks
    order = list(range(first_query, chunks)) + list(range(first_query))

    start_all(over(True, z))
    pl.when(z < last)(lambda: start_all(up(True, z)))
    pl.when(z > 0)(lambda: start_all(down(True, z)))
    for chunk in order:
        hidden_copy(0, chunk).start()
    for chunk in order:
        hidden_copy(1, chunk).start()

    gains[...] = gain[...].astype(f32).reshape(gains.shape)
    docs = count[0]
    positions = [home[ids[0, j]] for j in range(MAXDOC)]
    table_rows = hidden_rows.shape[0]
    hits = jnp.zeros((table_rows, SPAN), f32)
    for r in range(recompute.shape[0]):
        row = recompute[r:r + 1, :]
        doc_match = lax.broadcasted_iota(jnp.int32, (table_rows, CHUNK), 0) == (row >> 8)
        row_match = lax.broadcasted_iota(jnp.int32, (SPAN, CHUNK), 0) == (row & 255)
        hits = hits + lax.dot_general(
            jnp.where(doc_match, 1.0, 0.0).astype(bf16), jnp.where(row_match, 1.0, 0.0).astype(bf16),
            (((1,), (1,)), ((), ())), preferred_element_type=f32,
        )
    dead = lax.broadcasted_iota(jnp.int32, (table_rows, SPAN), 0) >= docs
    hidden_rows[...] = jnp.where(jnp.logical_or(dead, hits > 0.5), MASKED, 0.0)
    top[...] = jnp.full(top.shape, MASKED, f32)
    total[...] = jnp.zeros(total.shape, f32)
    mixed[...] = jnp.zeros(mixed.shape, f32)

    local[0].wait()
    block = wide.shape[0]

    def split_pairs(i, carry):
        wide[...] = wkv_raw[pl.ds(pl.multiple_of(i * block, block), block), :].astype(f32)
        rows = pl.ds(pl.multiple_of(i * (block // 2), block // 2), block // 2)
        wkv[rows, 0:HEAD] = wide[pl.ds(0, block // 2, stride=2), :].astype(bf16)
        wkv[rows, HEAD:2 * HEAD] = wide[pl.ds(1, block // 2, stride=2), :].astype(bf16)
        return carry

    lax.fori_loop(0, wkv_raw.shape[0] // block, split_pairs, 0)
    for copy in local[1:]:
        copy.wait()

    parts, _, width = hid.shape
    heads = wq.shape[1] // HEAD
    own_slot = cached.shape[0] - 1

    def row_angles(chunk):
        if chunk >= first_query:
            offset = docs * SPAN + (chunk - first_query) * CHUNK
            place = lax.broadcasted_iota(jnp.int32, (CHUNK, HEAD), 0) + offset
            return place.astype(f32) * freq[...]
        row = jnp.broadcast_to(recompute[chunk:chunk + 1, :].astype(f32), (CHUNK, CHUNK))
        down_rows = lax.broadcasted_iota(jnp.int32, (CHUNK, CHUNK), 0)
        diagonal_entry = down_rows == lax.broadcasted_iota(jnp.int32, (CHUNK, CHUNK), 1)
        return jnp.sum(jnp.where(diagonal_entry, row, 0.0), axis=1, keepdims=True) * freq[...]

    def normalise(chunk, place):
        hidden_arrival(1, chunk)
        hidden_arrival(2, chunk)

        def some_rows(i, carry):
            rows = pl.ds(pl.multiple_of(chunk * CHUNK + i * NORM_ROWS, NORM_ROWS), NORM_ROWS)
            placed = pl.ds(pl.multiple_of(place * CHUNK + i * NORM_ROWS, NORM_ROWS), NORM_ROWS)
            squares = jnp.zeros((NORM_ROWS, HEAD), f32)
            for part in range(parts):
                for block in range(width // HEAD):
                    value = hid[part, rows, block * HEAD:(block + 1) * HEAD].astype(f32)
                    squares = squares + value * value
            mean = jnp.sum(squares, axis=1, keepdims=True) * (1.0 / (parts * width))
            inverse_rms = jnp.broadcast_to(lax.rsqrt(mean + norm_eps), (NORM_ROWS, HEAD))
            for part in range(parts):
                for block in range(width // HEAD):
                    first = part * width + block * HEAD
                    value = hid[part, rows, block * HEAD:(block + 1) * HEAD].astype(f32)
                    value = value * inverse_rms * gains[:, first:first + HEAD]
                    normed[placed, first:first + HEAD] = value.astype(bf16)
            return carry

        lax.fori_loop(0, CHUNK // NORM_ROWS, some_rows, 0)

    def project(group):
        for n, chunk in enumerate(group):
            normalise(chunk, n)
        ready = normed[0:len(group) * CHUNK, :]
        kv_all = jnp.dot(ready, wkv[...], preferred_element_type=f32)
        is_query = group[0] >= first_query
        if is_query:
            q_all = jnp.dot(ready, wq[...], preferred_element_type=f32)
        per_span = SPAN // CHUNK
        for n, chunk in enumerate(group):
            rows = pl.ds(chunk * CHUNK, CHUNK)
            here = slice(n * CHUNK, (n + 1) * CHUNK)
            angle = row_angles(chunk)
            cosine, sine = jnp.cos(angle), jnp.sin(angle)
            sine = jnp.where(lax.broadcasted_iota(jnp.int32, angle.shape, 1) < HALF, -sine, sine)
            new_key = rotate(kv_all[here, :HEAD], cosine, sine).astype(bf16)
            new_value = kv_all[here, HEAD:].astype(bf16)
            place = pl.ds(chunk % per_span * CHUNK, CHUNK)
            cached[own_slot, chunk // per_span, 0, place, :] = new_key
            cached[own_slot, chunk // per_span, 1, place, :] = new_value
            if is_query:
                for g in range(heads):
                    q_rows = pl.ds(g * SPAN + (chunk - first_query) * CHUNK, CHUNK)
                    q = q_all[here, g * HEAD:(g + 1) * HEAD]
                    queries[q_rows, :] = rotate(q, cosine, sine).astype(bf16)
            else:
                fresh_out[rows, :HEAD] = new_key
                fresh_out[rows, HEAD:] = new_value

    exponent = HEAD ** (-0.5) * LOG2E
    query_block = scores.shape[1]

    def attend_group(slot, bias, causal):
        def some_queries(n, carry):
            rows = pl.ds(pl.multiple_of(n * query_block, query_block), query_block)
            q = queries[rows, :]
            before = top[rows, :]
            peak = before
            for i in range(stored):
                part = lax.dot_general(
                    q, cached[slot, i, 0], (((1,), (1,)), ((), ())), preferred_element_type=f32
                )
                if bias is not None:
                    part = part + bias[i]
                elif causal and i == stored - 1:
                    query_index = lax.broadcasted_iota(jnp.int32, (query_block, SPAN), 0) & (SPAN - 1)
                    key_index = lax.broadcasted_iota(jnp.int32, (query_block, SPAN), 1)
                    part = jnp.where(key_index <= query_index, part, MASKED)
                scores[i] = part
                peak = jnp.maximum(peak, jnp.maximum(part[:, :HEAD], part[:, HEAD:]))
            peak = jnp.broadcast_to(jnp.max(peak, axis=1, keepdims=True), (query_block, HEAD))
            top[rows, :] = peak
            fade = jnp.exp2((before - peak) * exponent)
            sums = total[rows, :] * fade
            gained = jnp.zeros((query_block, HEAD), f32)
            for i in range(stored):
                low = jnp.exp2((scores[i, :, :HEAD] - peak) * exponent)
                high = jnp.exp2((scores[i, :, HEAD:] - peak) * exponent)
                sums = sums + (low + high)
                weights = jnp.concatenate([low.astype(bf16), high.astype(bf16)], axis=1)
                gained = gained + jnp.dot(weights, cached[slot, i, 1], preferred_element_type=f32)
            total[rows, :] = sums
            mixed[rows, :] = mixed[rows, :] * fade + gained
            return carry

        lax.fori_loop(0, queries.shape[0] // query_block, some_queries, 0)

    def keep_cached(slot):
        return pltpu.make_async_copy(cached.at[slot], cached_out.at[slot], cached_sem.at[slot])

    def span_group(slot):
        bias = []
        for i in range(stored):
            position = slot * stored + i
            doc = table_rows - 1
            for j in range(MAXDOC):
                doc = doc + jnp.where(positions[j] == position, j - (table_rows - 1), 0)
            doc = jnp.clip(doc, 0, table_rows - 1)
            cosine, sine = doc_cos[pl.ds(doc, 1), :], doc_sin[pl.ds(doc, 1), :]
            bias.append(hidden_rows[pl.ds(doc, 1), :])
            for b in range(blocks):
                rows = slice(b * SB, (b + 1) * SB)
                first = i * 2 * blocks + b
                k = codes_all[slot, i, 0, rows, :].astype(f32) * scales_all[slot, first:first + 1, :]
                cached[slot, i, 0, rows, :] = rotate(k, cosine, sine).astype(bf16)
                first = first + blocks
                v = codes_all[slot, i, 1, rows, :].astype(f32) * scales_all[slot, first:first + 1, :]
                cached[slot, i, 1, rows, :] = v.astype(bf16)
        keep_cached(slot).start()
        attend_group(slot, bias, False)

    def span_step(k):
        @pl.when(z >= k)
        def _():
            for copy in up(False, z - k):
                copy.wait_recv()
            start_all(over(False, z - k))
            pl.when(z < last)(lambda: start_all(up(False, z - k)))

        @pl.when(z + k <= last)
        def _():
            for copy in down(False, z + k):
                copy.wait_recv()
            start_all(over(False, z + k))
            pl.when(z > 0)(lambda: start_all(down(False, z + k)))

    folded = jnp.where(z < 2, z, last - z)

    def near(k):
        owner = jnp.where(folded == 0, k, (1, 0, 2, 3)[k])
        return jnp.where(z < 2, owner, last - owner)

    def same_column(k):
        span_group(near(k) * 2 + x)

    def other_column(k):
        for copy in span_copies(False, near(k), 1 - x, x_send, x_recv, x_peer):
            copy.wait_recv()
        span_group(near(k) * 2 + 1 - x)

    def relay(i):
        hidden_arrival(0, order[i])
        hidden_copy(2, order[i]).start()

    scales_all[s] = scales_own[...]
    relay(0)
    span_step(1)
    relay(1)
    project(order[0:2])
    same_column(0)
    relay(2)
    span_step(2)
    other_column(0)
    same_column(1)
    relay(3)
    span_step(3)
    project(order[2:4])
    other_column(1)
    relay(4)
    same_column(2)
    same_column(3)
    project(order[4:5])
    other_column(2)
    relay(5)
    project(order[5:6])
    attend_group(own_slot, None, True)
    other_column(3)

    live = lax.broadcasted_iota(jnp.int32, (SPAN, HEAD), 0) < query_len[0]
    for g in range(heads):
        rows = pl.ds(g * SPAN, SPAN)
        result = mixed[rows, :] / jnp.sum(total[rows, :], axis=1, keepdims=True)
        attn_out[:, g * HEAD:(g + 1) * HEAD] = jnp.where(live, result, 0.0).astype(bf16)

    for slot in range(own_slot):
        keep_cached(slot).wait()
    for chunk in range(chunks):
        for kind in range(3):
            hidden_copy(kind, chunk).wait_send()
    for owner in range(4):
        for copy in over(False, owner):
            copy.wait_send()

        @pl.when(jnp.logical_and(z < last, owner <= z))
        def _():
            for copy in up(False, owner):
                copy.wait_send()

        @pl.when(jnp.logical_and(z > 0, owner >= z))
        def _():
            for copy in down(False, owner):
                copy.wait_send()


def stream(peers, tp, home, ids, count, query_len, hidden, codes, scales, w_q, w_kv, gain, recompute):
    rows, width = hidden.shape
    features = w_q.shape[0]
    heads = w_q.shape[1] // HEAD
    chunks = rows // CHUNK
    table_rows = 32
    doc_cos, doc_sin = doc_tables(table_rows)
    fresh = rows - SPAN
    dma = pltpu.SemaphoreType.DMA
    return pl.pallas_call(
        stream_kernel,
        out_shape=(
            jax.ShapeDtypeStruct((SPAN, heads * HEAD), bf16),
            jax.ShapeDtypeStruct((fresh, 2 * HEAD), bf16),
            jax.ShapeDtypeStruct((peers,) + codes.shape, bf16),
        ),
        in_specs=[SMEM] * 4 + [ANY, ANY, VMEM, ANY, ANY] + [VMEM] * 5,
        out_specs=(VMEM, VMEM, ANY),
        scratch_shapes=[
            pltpu.VMEM((tp, rows, width), bf16),
            pltpu.VMEM((features, w_q.shape[1]), bf16),
            pltpu.VMEM((2 * features, HEAD), bf16),
            pltpu.VMEM((features, 2 * HEAD), bf16),
            pltpu.VMEM((512, HEAD), f32),
            pltpu.VMEM((peers,) + codes.shape, bf16),
            pltpu.VMEM((SCALE_ROWS, HEAD), f32),
            pltpu.VMEM((peers, SCALE_ROWS, HEAD), f32),
            pltpu.VMEM((peers + 1,) + codes.shape, bf16),
            pltpu.VMEM((heads * SPAN, HEAD), bf16),
            pltpu.VMEM((codes.shape[0], 2 * SPAN, SPAN), f32),
            pltpu.VMEM((SPAN, features), bf16),
            pltpu.VMEM((1, features), f32),
            pltpu.VMEM((heads * SPAN, HEAD), f32),
            pltpu.VMEM((heads * SPAN, HEAD), f32),
            pltpu.VMEM((heads * SPAN, HEAD), f32),
            pltpu.VMEM((table_rows, SPAN), f32),
            dma((4,)),
            dma((peers,)),
            dma((3, chunks)),
            dma((3, chunks)),
            dma((4, 2)),
            dma((4, 2)),
            dma((4, 2)),
            dma((4, 2)),
            dma((4, 2)),
        ],
        compiler_params=pltpu.CompilerParams(
            collective_id=0, has_side_effects=True, vmem_limit_bytes=60 * 2**20
        ),
        name="stream_attend",
    )(home, ids, count, query_len, hidden, codes, scales, w_q, w_kv, gain, recompute,
      inverse_freq()[None, :], doc_cos, doc_sin)


def place_kernel(
    home, ids, count, recompute, attended, cached, fresh,
    out, context,
    fetched, placed, fetch_sem, write_sem,
):
    docs = count[0]

    def fetch(j):
        return pltpu.make_async_copy(cached.at[home[ids[0, j]]], fetched.at[j], fetch_sem.at[j])

    def write(j, part):
        rows = pl.ds(pl.multiple_of(j * SPAN, SPAN), SPAN)
        return pltpu.make_async_copy(placed.at[j, part], context.at[part, rows], write_sem.at[j, part])

    lax.fori_loop(0, docs, lambda j, n: (fetch(j).start(), n)[1], 0)
    out[...] = attended[...]
    ones = jnp.ones((fresh.shape[0], HEAD), bf16)

    def fill(j, carry):
        @pl.when(j < docs)
        def _():
            rows = lax.broadcasted_iota(jnp.int32, (SPAN, CHUNK), 0) + j * SPAN
            match = jnp.concatenate(
                [
                    jnp.where(recompute[r:r + 1, :] == rows, 1.0, 0.0).astype(bf16)
                    for r in range(recompute.shape[0])
                ],
                axis=1,
            )
            hit = jnp.dot(match, ones, preferred_element_type=f32) > 0.5
            patch = jnp.dot(match, fresh[...], preferred_element_type=f32)
            fetch(j).wait()
            for part in range(2):
                new = patch[:, part * HEAD:(part + 1) * HEAD]
                placed[j, part] = jnp.where(hit, new, fetched[j, part].astype(f32)).astype(bf16)

        @pl.when(j >= docs)
        def _():
            placed[j] = jnp.zeros(placed.shape[1:], bf16)

        write(j, 0).start()
        write(j, 1).start()
        return carry

    lax.fori_loop(0, MAXDOC, fill, 0)

    def drain(j, carry):
        write(j, 0).wait()
        write(j, 1).wait()
        return carry

    lax.fori_loop(0, MAXDOC, drain, 0)


def place(home, ids, count, recompute, attended, cached, fresh):
    context_max = MAXDOC * SPAN
    return pl.pallas_call(
        place_kernel,
        out_shape=(
            jax.ShapeDtypeStruct(attended.shape, bf16),
            jax.ShapeDtypeStruct((2, context_max, HEAD), bf16),
        ),
        in_specs=[SMEM] * 3 + [VMEM, VMEM, ANY, VMEM],
        out_specs=(VMEM, ANY),
        scratch_shapes=[
            pltpu.VMEM((MAXDOC, 2, SPAN, HEAD), bf16),
            pltpu.VMEM((MAXDOC, 2, SPAN, HEAD), bf16),
            pltpu.SemaphoreType.DMA((MAXDOC,)),
            pltpu.SemaphoreType.DMA((MAXDOC, 2)),
        ],
        compiler_params=pltpu.CompilerParams(vmem_limit_bytes=60 * 2**20),
        name="place_context",
    )(home, ids, count, recompute, attended, cached, fresh)


def plain_gather_and_project(hidden, codes, scales, w_q, w_kv, gain, angles):
    rows = hidden.shape[0]
    heads = w_q.shape[1] // HEAD
    all_codes = lax.all_gather(codes, "store", axis=0)
    all_scales = lax.all_gather(scales, "store", axis=0)
    features = lax.all_gather(hidden, "tp", axis=1, tiled=True).astype(f32)
    inverse_rms = lax.rsqrt(jnp.mean(features * features, axis=-1, keepdims=True) + norm_eps)
    normed = (features * inverse_rms * gain).astype(bf16)
    cosine, sine = jnp.cos(angles), jnp.sin(angles)
    sine = jnp.where(jnp.arange(HEAD)[None, :] < HALF, -sine, sine)
    kv = jnp.dot(normed, w_kv.reshape(-1, 2 * HEAD), preferred_element_type=f32)
    q = jnp.dot(normed[rows - SPAN:], w_q, preferred_element_type=f32)
    q = jnp.transpose(q.reshape(SPAN, heads, HEAD), (1, 0, 2))

    def turn(values, cosine, sine):
        return values * cosine + jnp.roll(values, HALF, axis=-1) * sine

    new_keys = turn(kv[:, :HEAD], cosine, sine)
    q = turn(q, cosine[rows - SPAN:], sine[rows - SPAN:]).astype(bf16)
    return q, new_keys, kv[:, HEAD:], all_codes, all_scales


def attend_kernel(
    stored, home, ids, count, recompute, query_len, codes, scales, doc_cos, doc_sin, q, new_k, new_v,
    out, context,
    fetched, scale_rows, key_rows, value_rows, keys, values, scores, top, total, mixed, fetch_sem, out_sem,
):
    docs = count[0]
    recompute_total = recompute.shape[0]
    context_max = MAXDOC * SPAN
    heads = q.shape[0]

    def fetch(j):
        position = home[ids[0, j]]
        return pltpu.make_async_copy(codes.at[position], fetched.at[j], fetch_sem.at[j])

    lax.fori_loop(0, docs, lambda j, n: (fetch(j).start(), n)[1], 0)
    scale_rows[...] = scales[...].astype(f32)

    def dequantise(j, carry):
        base = pl.multiple_of(j * SPAN, SPAN)

        @pl.when(j < docs)
        def _():
            fetch(j).wait()
            position = home[ids[0, j]]
            first = (position // stored) * SCALE_ROWS + (position % stored) * 4
            cosine, sine = doc_cos[pl.ds(j, 1), :], doc_sin[pl.ds(j, 1), :]
            for b in range(SPAN // SB):
                rows = pl.ds(base + b * SB, SB)
                k = fetched[j, 0, b * SB:(b + 1) * SB, :].astype(f32) * scale_rows[pl.ds(first + b, 1), :]
                key_rows[rows, :] = rotate(k, cosine, sine)
                v = fetched[j, 1, b * SB:(b + 1) * SB, :].astype(f32) * scale_rows[pl.ds(first + 2 + b, 1), :]
                value_rows[rows, :] = v

        @pl.when(j >= docs)
        def _():
            key_rows[pl.ds(base, SPAN), :] = jnp.zeros((SPAN, HEAD), f32)
            value_rows[pl.ds(base, SPAN), :] = jnp.zeros((SPAN, HEAD), f32)

        return carry

    lax.fori_loop(0, MAXDOC, dequantise, 0)

    def patch(i, carry):
        for u in range(8):
            source = i * 8 + u
            row = recompute[source]
            key_rows[pl.ds(row, 1), :] = new_k[pl.ds(source, 1), :]
            value_rows[pl.ds(row, 1), :] = new_v[pl.ds(source, 1), :]
        return carry

    lax.fori_loop(0, recompute_total // 8, patch, 0)

    def narrow(j, carry):
        rows = pl.ds(pl.multiple_of(j * SPAN, SPAN), SPAN)
        keys[rows, :] = key_rows[rows, :].astype(bf16)
        values[rows, :] = value_rows[rows, :].astype(bf16)
        return carry

    lax.fori_loop(0, MAXDOC, narrow, 0)
    keys[context_max:context_max + SPAN, :] = new_k[recompute_total:, :].astype(bf16)
    values[context_max:context_max + SPAN, :] = new_v[recompute_total:, :].astype(bf16)
    writes = [
        pltpu.make_async_copy(keys.at[0:context_max], context.at[0], out_sem.at[0]),
        pltpu.make_async_copy(values.at[0:context_max], context.at[1], out_sem.at[1]),
    ]
    for copy in writes:
        copy.start()

    def score(g, rows):
        return lax.dot_general(q[g], keys[rows, :], (((1,), (1,)), ((), ())), preferred_element_type=f32)

    own_rows = pl.ds(context_max, SPAN)
    query_index = lax.broadcasted_iota(jnp.int32, (SPAN, SPAN), 0)
    key_index = lax.broadcasted_iota(jnp.int32, (SPAN, SPAN), 1)
    for g in range(heads):
        own = jnp.where(key_index <= query_index, score(g, own_rows), -1e30)
        scores[MAXDOC, g] = own
        top[g] = jnp.maximum(own[:, :HEAD], own[:, HEAD:])

    def first_pass(j, carry):
        rows = pl.ds(pl.multiple_of(j * SPAN, SPAN), SPAN)
        for g in range(heads):
            block = score(g, rows)
            scores[j, g] = block
            top[g] = jnp.maximum(top[g], jnp.maximum(block[:, :HEAD], block[:, HEAD:]))
        return carry

    lax.fori_loop(0, docs, first_pass, 0)
    for g in range(heads):
        top[g] = jnp.broadcast_to(jnp.max(top[g], axis=1, keepdims=True), (SPAN, HEAD))
        total[g] = jnp.zeros((SPAN, HEAD), f32)
        mixed[g] = jnp.zeros((SPAN, HEAD), f32)

    def weigh(slot, rows):
        for g in range(heads):
            peak = top[g]
            low = jnp.exp((scores[slot, g, :, :HEAD] - peak) * HEAD ** (-0.5))
            high = jnp.exp((scores[slot, g, :, HEAD:] - peak) * HEAD ** (-0.5))
            total[g] += low + high
            weights = jnp.concatenate([low.astype(bf16), high.astype(bf16)], axis=1)
            mixed[g] += jnp.dot(weights, values[rows, :], preferred_element_type=f32)

    def second_pass(j, carry):
        weigh(j, pl.ds(pl.multiple_of(j * SPAN, SPAN), SPAN))
        return carry

    lax.fori_loop(0, docs, second_pass, 0)
    weigh(MAXDOC, own_rows)
    live = lax.broadcasted_iota(jnp.int32, (SPAN, HEAD), 0) < query_len[0]
    for g in range(heads):
        result = mixed[g] / jnp.sum(total[g], axis=1, keepdims=True)
        out[:, g * HEAD:(g + 1) * HEAD] = jnp.where(live, result, 0.0).astype(bf16)
    for copy in writes:
        copy.wait()


def attend(stored, home, ids, count, recompute, query_len, codes, scales, q, new_k, new_v):
    context_max = MAXDOC * SPAN
    heads = q.shape[0]
    freq = inverse_freq()
    angle = ((np.arange(24) * SPAN).astype(np.float32)[:, None] * freq[None, :]).astype(np.float64)
    sign = np.where(np.arange(HEAD) < HALF, -1.0, 1.0)
    doc_cos = np.cos(angle).astype(np.float32)
    doc_sin = (np.sin(angle) * sign).astype(np.float32)
    return pl.pallas_call(
        functools.partial(attend_kernel, stored),
        out_shape=(
            jax.ShapeDtypeStruct((SPAN, heads * HEAD), bf16),
            jax.ShapeDtypeStruct((2, context_max, HEAD), bf16),
        ),
        in_specs=[SMEM] * 5 + [ANY] + [VMEM] * 6,
        out_specs=(VMEM, ANY),
        scratch_shapes=[
            pltpu.VMEM((MAXDOC, 2, SPAN, HEAD), bf16),
            pltpu.VMEM(scales.shape, f32),
            pltpu.VMEM((context_max, HEAD), f32),
            pltpu.VMEM((context_max, HEAD), f32),
            pltpu.VMEM((context_max + SPAN, HEAD), bf16),
            pltpu.VMEM((context_max + SPAN, HEAD), bf16),
            pltpu.VMEM((MAXDOC + 1, heads, SPAN, SPAN), f32),
            pltpu.VMEM((heads, SPAN, HEAD), f32),
            pltpu.VMEM((heads, SPAN, HEAD), f32),
            pltpu.VMEM((heads, SPAN, HEAD), f32),
            pltpu.SemaphoreType.DMA((MAXDOC,)),
            pltpu.SemaphoreType.DMA((2,)),
        ],
        compiler_params=pltpu.CompilerParams(vmem_limit_bytes=48 * 2**20),
        name="patch_attend",
    )(home, ids, count, recompute, query_len, codes, scales, doc_cos, doc_sin, q, new_k, new_v)


def on_device(
    kv_store, kv_scale, span_home, doc_ids, doc_count, recompute_rows, query_len, hidden, norm_gain, w_q, w_kv,
):
    peers, tp = lax.axis_size("store"), lax.axis_size("tp")
    stored = kv_store.shape[0]
    gain = norm_gain.astype(f32).reshape(1, -1)
    pairs = w_kv.reshape(-1, HEAD)
    if (peers, tp) == (8, 4):
        attended, fresh, cached = stream(
            peers, tp, span_home, doc_ids, doc_count, query_len, hidden[0], kv_store,
            jnp.transpose(kv_scale, (2, 1, 3, 0)), w_q, pairs, norm_gain, recompute_rows[0],
        )
        cached = cached.reshape((peers * stored,) + kv_store.shape[1:])
        attention, context = place(
            span_home, doc_ids, doc_count, recompute_rows[0], attended, cached, fresh
        )
        return attention[None], context[None]
    scales = jnp.broadcast_to(kv_scale.reshape(stored * 4, 1), (stored * 4, HEAD))
    scales = jnp.pad(scales, ((0, SCALE_ROWS - stored * 4), (0, 0)))
    flat = recompute_rows.reshape(-1)
    row_pos = jnp.concatenate([flat, doc_count[0] * SPAN + jnp.arange(SPAN, dtype=jnp.int32)])
    angles = row_pos.astype(f32)[:, None] * inverse_freq()[None, :]
    gathered = plain_gather_and_project(hidden[0], kv_store, scales, w_q, pairs, gain, angles)
    q, new_k, new_v, codes, all_scales = gathered
    attention, context = attend(
        stored, span_home, doc_ids, doc_count, flat, query_len,
        codes.reshape((peers * stored,) + kv_store.shape[1:]), all_scales.reshape(-1, HEAD), q, new_k, new_v,
    )
    return attention[None], context[None]


def solution(mesh):
    placed = (
        P("store", None, None, "tp"),
        P("store", None, "tp", None),
        P(),
        P("store", None),
        P("store"),
        P("store", None, None),
        P("store"),
        P("store", None, "tp"),
        P(),
        P(None, "tp"),
        P(None, None, "tp"),
    )
    return jax.shard_map(
        on_device,
        mesh=mesh,
        in_specs=placed,
        out_specs=(P("store", None, "tp"), P("store", None, None, "tp")),
        check_vma=False,
    )
```
